32 devices in a mesh: spec: 4 (over y, core), pix: 8 (over z, x).
Axes of the slice: x: 2, y: 2, z: 4, core: 2. Of those that a mesh axis runs over, the one named last changes fastest.
Arguments:
- spectra_flux: float32 [768, 4096], P('spec', 'pix'), may hold values from -8 to 8
- pixel_weights: float32 [768, 4096], P('spec', 'pix'), may hold values from 0.05 to 20
- old_basis: float32 [32, 4096], P(None, 'pix'), may hold values from -3 to 3
Outputs:
- new_basis: float32 [32, 4096], P(None, 'pix')
The draws below stay inside these ranges and needn't reach their ends.
All inputs are finite; a program needn't handle non-finite values.
Results may differ from the reference program's by a relative error of at most 0.0003.
Values sent between devices are 32-bit elements; how exact they have to be, the bound alone decides.
No kernel may reach another device: no remote copies, remote signals or barrier semaphores. Data moves between devices by JAX's collectives and lax.ppermute only.
A program may use at most 64 MiB of HBM per device.

```python
import math
import jax
import jax.numpy as jnp
from jax import lax

K = 32
NS = 768
NP = 4096


def class_tables(key):
    spec_class = jax.random.randint(jax.random.fold_in(key, 101), (NS,), 0, K)
    pix_class = jax.random.randint(jax.random.fold_in(key, 102), (NP,), 0, K)
    return (spec_class, pix_class)


def orthonormal(key):
    random_matrix = jax.random.normal(key, (K, K), jnp.float32)
    columns = []
    for column_pos in range(K):
        vector = random_matrix[:, column_pos]
        for repeat in range(2):
            for earlier in columns:
                vector = vector - jnp.dot(earlier, vector, precision=lax.Precision.HIGHEST) * earlier
        vector = vector / jnp.sqrt(jnp.sum(vector * vector))
        columns.append(vector)
    return jnp.stack(columns, axis=1)


def basis_from(key):
    spec_class, pix_class = class_tables(key)
    rotation = orthonormal(jax.random.fold_in(key, 105))
    flips = jax.random.bernoulli(jax.random.fold_in(key, 106), 0.5, (NP,))
    pix_signs = jnp.where(flips, 1.0, -1.0).astype(jnp.float32)
    jitter = jnp.clip(jax.random.normal(jax.random.fold_in(key, 108), (K, NP), jnp.float32), -6.0, 6.0)
    return 1.5 * rotation[:, pix_class] * pix_signs[None, :] + 0.2 * jitter


def draw_old_basis(key, part):
    return basis_from(key)


def draw_pixel_weights(key, part):
    spec_class, pix_class = class_tables(key)
    levels = jax.random.uniform(jax.random.fold_in(key, 103), (K, K), jnp.float32, -1.0, 1.0)
    lookup = levels[spec_class][:, pix_class]
    roughness = math.log(2.0) * jax.random.uniform(jax.random.fold_in(key, 104), (NS, NP), jnp.float32, -1.0, 1.0)
    return jnp.exp(math.log(10.0) * lookup + roughness)


def draw_spectra_flux(key, part):
    spec_class, pix_class = class_tables(key)
    basis_rows = basis_from(key)
    turning = orthonormal(jax.random.fold_in(key, 107))
    coefficients = 2.0 * turning[:, spec_class]
    clean_flux = jnp.dot(coefficients.T, basis_rows, precision=lax.Precision.HIGHEST)
    jitter = jnp.clip(jax.random.normal(jax.random.fold_in(key, 109), (NS, NP), jnp.float32), -4.0, 4.0)
    return jnp.clip(clean_flux + 0.5 * jitter, -8.0, 8.0)


def setup_inputs(seed: int = 0) -> dict:
    keys = jax.random.split(jax.random.key(seed), 4)
    return {
        "spectra_flux": draw_spectra_flux(jax.random.fold_in(keys[3], 71), 0),
        "pixel_weights": draw_pixel_weights(jax.random.fold_in(keys[3], 71), 0),
        "old_basis": draw_old_basis(jax.random.fold_in(keys[3], 71), 0),
    }


def outer_rows(factors):
    extent = factors.shape[0]
    return (factors[:, None, :] * factors[None, :, :]).reshape(extent * extent, -1)

def solve_batch(matrix_flat, target):
    extent = target.shape[0]
    matrix = matrix_flat.reshape(extent, extent, -1)
    row_index = lax.broadcasted_iota(jnp.int32, (extent, 1), 0)
    factor = jnp.zeros_like(matrix)
    for column_pos in range(extent):
        partial_sum = matrix[:, column_pos, :] - lax.optimization_barrier(jnp.sum(factor * factor[:, column_pos:column_pos + 1, :], axis=0))
        pivot_val = jnp.sqrt(partial_sum[column_pos])
        column = jnp.where(row_index >= column_pos, partial_sum / pivot_val, jnp.zeros_like(partial_sum))
        factor = factor.at[column_pos].set(column)
    forward = jnp.zeros_like(target)
    for column_pos in range(extent):
        value = (target[column_pos] - lax.optimization_barrier(jnp.sum(factor[:, column_pos, :] * forward, axis=0))) / factor[column_pos, column_pos]
        forward = forward.at[column_pos].set(value)
    solved = jnp.zeros_like(target)
    for column_pos in reversed(range(extent)):
        value = (forward[column_pos] - lax.optimization_barrier(jnp.sum(factor[column_pos] * solved, axis=0))) / factor[column_pos, column_pos]
        solved = solved.at[column_pos].set(value)
    return solved

def contract_last(left, right):
    return lax.dot_general(left, right, (((1,), (1,)), ((), ())), precision=lax.Precision.HIGHEST)

def reference(spectra_flux, pixel_weights, old_basis):
    weighted = pixel_weights * spectra_flux
    spec_gram = contract_last(outer_rows(old_basis), pixel_weights)
    spec_target = contract_last(old_basis, weighted)
    coeffs = solve_batch(spec_gram, spec_target)
    pix_gram = jnp.dot(outer_rows(coeffs), pixel_weights, precision=lax.Precision.HIGHEST)
    pix_target = jnp.dot(coeffs, weighted, precision=lax.Precision.HIGHEST)
    return solve_batch(pix_gram, pix_target)
```

```python
import functools

import jax
import jax.numpy as jnp
from jax import lax
from jax.experimental import pallas as pl
from jax.experimental.pallas import tpu as pltpu
from jax.sharding import PartitionSpec as P

LANES = 128
ROWS = 8
VMEM = pl.BlockSpec(memory_space=pltpu.VMEM)
SMEM = pl.BlockSpec(memory_space=pltpu.SMEM)
LIMIT = 48 * 1024 * 1024


def up(value, multiple):
    return -(-value // multiple) * multiple


def pair_rows(rank):
    return rank * (rank // 2) + rank // 2


def write_pairs(twice, pairs, rank):
    first = twice[0:rank, :]
    for diag in range(rank // 2):
        pairs[diag * rank : (diag + 1) * rank, :] = first * twice[diag : diag + rank, :]
    half = rank // 2
    pairs[half * rank : half * rank + half, :] = first[0:half] * first[half:rank]


def unpack(packed, full, rank):
    for diag in range(rank // 2 + 1):
        base = diag * rank
        count = rank if diag < rank // 2 else rank // 2
        wrap = min(count, rank - diag)
        part = packed[base : base + wrap, :]
        full[pl.ds(diag, wrap, stride=rank + 1), :] = part
        if diag:
            full[pl.ds(diag * rank, wrap, stride=rank + 1), :] = part
        if wrap < count:
            part = packed[base + wrap : base + count, :]
            full[pl.ds(rank - diag, count - wrap, stride=rank + 1), :] = part
            full[pl.ds((rank - diag) * rank, count - wrap, stride=rank + 1), :] = part


def solve(full, target, scaled, rank):
    row = lax.broadcasted_iota(jnp.int32, target.shape, 0)
    pivots = jnp.zeros_like(target)
    for k in range(rank):
        column = full[k * rank : (k + 1) * rank, :]
        for j in range(k):
            column = column - scaled[j * rank : (j + 1) * rank, :] * full[j * rank + k : j * rank + k + 1, :]
        full[k * rank : (k + 1) * rank, :] = column
        here = row == k
        factor = jnp.where(here, 0.0, column * (1.0 / column[k : k + 1, :]))
        scaled[k * rank : (k + 1) * rank, :] = factor
        pivots = jnp.where(here, column, pivots)
        target = target - factor * target[k : k + 1, :]
    return target / pivots


def dot(left, right, right_axis):
    return lax.dot_general(
        left,
        right,
        (((1,), (right_axis,)), ((), ())),
        precision=lax.Precision.HIGHEST,
        preferred_element_type=jnp.float32,
    )


def spec_kernel(me, flux, weights, basis, gram, *rest, peers, chunk):
    picks, (twice, pairs) = rest[:peers], rest[peers:]
    rank, pixels = basis.shape
    share = pixels // peers
    lead = pair_rows(rank)
    twice[0:rank, :] = basis[...]
    twice[rank:, :] = basis[...]
    write_pairs(twice, pairs, rank)
    weighted = weights[...] * flux[...]
    packed = dot(weights[...], pairs[...], 1)
    target = dot(weighted, basis[...], 1)
    for k in range(gram.shape[0]):
        gram[k, 0:chunk, 0:lead] = packed[k * chunk : (k + 1) * chunk, :]
        gram[k, 0:chunk, lead : lead + rank] = target[k * chunk : (k + 1) * chunk, :]
    for q in range(peers):
        start = (me[0] ^ q) * share
        if share % LANES == 0:
            start = pl.multiple_of(start, LANES)
            picks[q][0] = weights[:, pl.ds(start, share)]
            picks[q][1] = weights[:, pl.ds(start, share)] * flux[:, pl.ds(start, share)]
        else:
            for s in range(peers):

                @pl.when(me[0] ^ q == s)
                def _():
                    picks[q][0] = weights[:, s * share : (s + 1) * share]
                    picks[q][1] = weighted[:, s * share : (s + 1) * share]


def coeff_kernel(parts, out, packed, full, scaled, *, rank, chunk):
    total = parts[0]
    for k in range(1, parts.shape[0]):
        total = total + parts[k]
    rows = total.shape[0]
    square = jnp.concatenate([total, jnp.ones((LANES - rows, total.shape[1]), jnp.float32)], axis=0)
    for k in range(total.shape[1] // LANES):
        packed[k * LANES : (k + 1) * LANES, :] = square[:, k * LANES : (k + 1) * LANES].T
    lead = pair_rows(rank)
    unpack(packed, full, rank)
    solved = solve(full, packed[lead : lead + rank, :], scaled, rank)
    lane = lax.broadcasted_iota(jnp.int32, (ROWS, LANES), 1)
    tile = jnp.zeros((ROWS, LANES), jnp.float32)
    for a in range(rank // ROWS):
        part = solved[a * ROWS : (a + 1) * ROWS, :]
        if a:
            part = pltpu.roll(part, a * chunk, 1)
        tile = jnp.where((lane >= a * chunk) & (lane < (a + 1) * chunk), part, tile)
    for k in range(out.shape[0]):
        out[k] = tile


def pixel_kernel(me, tiles, *rest, peers, rank, chunk):
    picks, (out, twice, pairs, both, full, scaled) = rest[:peers], rest[peers:]
    spectra = picks[0].shape[1]
    share = picks[0].shape[2]
    group = spectra // chunk
    lane = lax.broadcasted_iota(jnp.int32, (ROWS, LANES), 1)
    width = twice.shape[1]
    for q in range(peers):
        both[0, q * spectra : (q + 1) * spectra, :] = picks[q][0]
        both[1, q * spectra : (q + 1) * spectra, :] = picks[q][1]
    for a in range(rank // ROWS):
        columns = [jnp.zeros((ROWS, LANES), jnp.float32) for _ in range(width // LANES)]
        for q in range(peers):
            for k in range(group):
                part = tiles[(me[0] ^ q) * group + k]
                start = q * spectra + k * chunk
                shift = (start - a * chunk) % LANES
                if shift:
                    part = pltpu.roll(part, shift, 1)
                for t in range(start // LANES, (start + chunk - 1) // LANES + 1):
                    low, high = max(start - t * LANES, 0), min(start + chunk - t * LANES, LANES)
                    columns[t] = jnp.where((lane >= low) & (lane < high), part, columns[t])
        for t, column in enumerate(columns):
            twice[a * ROWS : (a + 1) * ROWS, t * LANES : (t + 1) * LANES] = column
            twice[rank + a * ROWS : rank + (a + 1) * ROWS, t * LANES : (t + 1) * LANES] = column
    write_pairs(twice, pairs, rank)
    depth = both.shape[1]
    packed = dot(pairs[:, 0:depth], both[0], 0)
    target = dot(twice[0:rank, 0:depth], both[1], 0)
    if share < LANES:
        filler = jnp.ones((packed.shape[0], LANES - share), jnp.float32)
        packed = jnp.concatenate([packed, filler], axis=1)
        target = jnp.concatenate([target, filler[0:rank]], axis=1)
    unpack(packed, full, rank)
    out[...] = solve(full, target, scaled, rank)[:, 0:share]


def place_kernel(me, *rest, peers):
    shares, out = rest[:peers], rest[peers]
    share = shares[0].shape[1]
    for q in range(peers):
        if share % LANES == 0:
            out[:, pl.ds(pl.multiple_of((me[0] ^ q) * share, LANES), share)] = shares[q][...]
        else:
            for s in range(peers):

                @pl.when(me[0] ^ q == s)
                def _():
                    out[:, s * share : (s + 1) * share] = shares[q][...]


def call(kernel, outs, scratch, *args, smem=0):
    return pl.pallas_call(
        kernel,
        out_shape=outs,
        in_specs=[SMEM] * smem + [VMEM] * (len(args) - smem),
        out_specs=jax.tree.map(lambda _: VMEM, outs),
        scratch_shapes=[pltpu.VMEM(shape, jnp.float32) for shape in scratch],
        compiler_params=pltpu.CompilerParams(vmem_limit_bytes=LIMIT),
    )(*args)


def shape(*sizes):
    return jax.ShapeDtypeStruct(sizes, jnp.float32)


def local(peers, groups, spectra_flux, pixel_weights, old_basis):
    spectra, pixels = pixel_weights.shape
    rank = old_basis.shape[0]
    share, chunk = pixels // peers, spectra // groups
    lead = pair_rows(rank)
    wide = up(lead + rank, LANES)
    me = lax.axis_index("spec").astype(jnp.int32).reshape(1)

    gram, *picks = call(
        functools.partial(spec_kernel, peers=peers, chunk=chunk),
        [shape(groups, up(chunk, ROWS), wide)] + [shape(2, spectra, share)] * peers,
        [(2 * rank, pixels), (lead, pixels)],
        me,
        spectra_flux,
        pixel_weights,
        old_basis,
        smem=1,
    )

    def swap(value, q):
        return lax.ppermute(value, "spec", [(s, s ^ q) for s in range(peers)])

    picks = [picks[0]] + [swap(picks[q], q) for q in range(1, peers)]
    parts = lax.all_to_all(gram, "pix", 0, 0)
    tiles = call(
        functools.partial(coeff_kernel, rank=rank, chunk=chunk),
        shape(peers * groups, ROWS, LANES),
        [(wide, LANES), (rank * rank, LANES), (rank * rank, LANES)],
        parts,
    )
    tiles = lax.all_to_all(tiles, ("spec", "pix"), 0, 0)
    depth = peers * spectra
    basis_share = call(
        functools.partial(pixel_kernel, peers=peers, rank=rank, chunk=chunk),
        shape(rank, share),
        [
            (2 * rank, up(depth, LANES)),
            (lead, up(depth, LANES)),
            (2, depth, share),
            (rank * rank, LANES),
            (rank * rank, LANES),
        ],
        me,
        tiles,
        *picks,
        smem=1,
    )
    shares = [basis_share] + [swap(basis_share, q) for q in range(1, peers)]
    return call(functools.partial(place_kernel, peers=peers), shape(rank, pixels), [], me, *shares, smem=1)


def solution(mesh):
    placed = (P("spec", "pix"), P("spec", "pix"), P(None, "pix"))
    body = functools.partial(local, mesh.shape["spec"], mesh.shape["pix"])
    return jax.shard_map(body, mesh=mesh, in_specs=placed, out_specs=P(None, "pix"), check_vma=False)
```

```python
import functools

import jax
import jax.numpy as jnp
from jax import lax
from jax.experimental import pallas as pl
from jax.experimental.pallas import tpu as pltpu
from jax.sharding import PartitionSpec as P

LANES = 128
ROWS = 8
VMEM = pl.BlockSpec(memory_space=pltpu.VMEM)
LIMIT = 48 * 1024 * 1024


def up(value, multiple):
    return -(-value // multiple) * multiple


def pair_rows(rank):
    return rank * (rank // 2) + rank // 2


def write_pairs(twice, pairs, rank):
    first = twice[0:rank, :]
    for diag in range(rank // 2):
        pairs[diag * rank : (diag + 1) * rank, :] = first * twice[diag : diag + rank, :]
    half = rank // 2
    pairs[half * rank : half * rank + half, :] = first[0:half] * first[half:rank]


def unpack(packed, full, rank):
    for diag in range(rank // 2 + 1):
        base = diag * rank
        count = rank if diag < rank // 2 else rank // 2
        wrap = min(count, rank - diag)
        part = packed[base : base + wrap, :]
        full[pl.ds(diag, wrap, stride=rank + 1), :] = part
        if diag:
            full[pl.ds(diag * rank, wrap, stride=rank + 1), :] = part
        if wrap < count:
            part = packed[base + wrap : base + count, :]
            full[pl.ds(rank - diag, count - wrap, stride=rank + 1), :] = part
            full[pl.ds((rank - diag) * rank, count - wrap, stride=rank + 1), :] = part


def solve(full, target, scaled, rank):
    row = lax.broadcasted_iota(jnp.int32, target.shape, 0)
    pivots = jnp.zeros_like(target)
    for k in range(rank):
        column = full[k * rank : (k + 1) * rank, :]
        for j in range(k):
            column = column - scaled[j * rank : (j + 1) * rank, :] * full[j * rank + k : j * rank + k + 1, :]
        full[k * rank : (k + 1) * rank, :] = column
        here = row == k
        factor = jnp.where(here, 0.0, column * (1.0 / column[k : k + 1, :]))
        scaled[k * rank : (k + 1) * rank, :] = factor
        pivots = jnp.where(here, column, pivots)
        target = target - factor * target[k : k + 1, :]
    return target / pivots


def dot(left, right, right_axis):
    return lax.dot_general(
        left,
        right,
        (((1,), (right_axis,)), ((), ())),
        precision=lax.Precision.HIGHEST,
        preferred_element_type=jnp.float32,
    )


def spec_kernel(flux_hbm, weights_hbm, basis_hbm, keep, send, own, other, *scratch, chunk):
    flux, weights, basis, twice, pairs, grams, sems = scratch
    copies = [
        pltpu.make_async_copy(source, target, sems.at[k])
        for k, (source, target) in enumerate(((basis_hbm, basis), (weights_hbm, weights), (flux_hbm, flux)))
    ]
    for copy in copies:
        copy.start()
    rank, pixels = basis.shape
    half = own.shape[2]
    lead = pair_rows(rank)
    copies[0].wait()
    twice[0:rank, :] = basis[...]
    twice[rank:, :] = basis[...]
    write_pairs(twice, pairs, rank)
    copies[1].wait()
    packed = dot(weights[...], pairs[...], 1)
    copies[2].wait()
    flux[...] = weights[...] * flux[...]
    target = dot(flux[...], basis[...], 1)
    for k in range(grams.shape[0]):
        grams[k, 0:chunk, 0:lead] = packed[k * chunk : (k + 1) * chunk, :]
        grams[k, 0:chunk, lead : lead + rank] = target[k * chunk : (k + 1) * chunk, :]
    for k in range(grams.shape[0] // 2):
        keep[k] = grams[lax.axis_index("pix") ^ (2 * k)]
        send[k] = grams[lax.axis_index("pix") ^ (2 * k + 1)]
    low = pl.multiple_of((lax.axis_index("spec") & 1) * half, LANES)
    high = pl.multiple_of(half - low, LANES)
    own[0] = weights[:, pl.ds(low, half)]
    own[1] = flux[:, pl.ds(low, half)]
    other[0] = weights[:, pl.ds(high, half)]
    other[1] = flux[:, pl.ds(high, half)]


def fold_kernel(keep, arrived, *outs):
    for k, out in enumerate(outs):
        out[...] = keep[k] + arrived[k]


def coeff_kernel(*refs, rank, chunk):
    parts, (out, packed, full, scaled) = refs[:-4], refs[-4:]
    total = parts[0][...]
    for part in parts[1:]:
        total = total + part[...]
    rows = total.shape[0]
    square = jnp.concatenate([total, jnp.ones((LANES - rows, total.shape[1]), jnp.float32)], axis=0)
    for k in range(total.shape[1] // LANES):
        packed[k * LANES : (k + 1) * LANES, :] = square[:, k * LANES : (k + 1) * LANES].T
    lead = pair_rows(rank)
    unpack(packed, full, rank)
    solved = solve(full, packed[lead : lead + rank, :], scaled, rank)
    lane = lax.broadcasted_iota(jnp.int32, (ROWS, LANES), 1)
    tile = jnp.zeros((ROWS, LANES), jnp.float32)
    for a in range(rank // ROWS):
        part = solved[a * ROWS : (a + 1) * ROWS, :]
        if a:
            part = pltpu.roll(part, a * chunk, 1)
        tile = jnp.where((lane >= a * chunk) & (lane < (a + 1) * chunk), part, tile)
    for k in range(out.shape[0]):
        out[k] = tile


def pixel_kernel(tiles, *rest, peers, rank, chunk):
    picks, (out, twice, pairs, both, full, scaled) = rest[:peers], rest[peers:]
    spectra = picks[0].shape[1]
    half = picks[0].shape[2]
    group = spectra // chunk
    lane = lax.broadcasted_iota(jnp.int32, (ROWS, LANES), 1)
    width = twice.shape[1]
    for q in range(peers):
        both[0, q * spectra : (q + 1) * spectra, :] = picks[q][0]
        both[1, q * spectra : (q + 1) * spectra, :] = picks[q][1]
    for a in range(rank // ROWS):
        columns = [jnp.zeros((ROWS, LANES), jnp.float32) for _ in range(width // LANES)]
        for q in range(peers):
            for k in range(group):
                part = tiles[(lax.axis_index("spec") ^ q) * group + k]
                start = q * spectra + k * chunk
                shift = (start - a * chunk) % LANES
                if shift:
                    part = pltpu.roll(part, shift, 1)
                for t in range(start // LANES, (start + chunk - 1) // LANES + 1):
                    low, high = max(start - t * LANES, 0), min(start + chunk - t * LANES, LANES)
                    columns[t] = jnp.where((lane >= low) & (lane < high), part, columns[t])
        for t, column in enumerate(columns):
            twice[a * ROWS : (a + 1) * ROWS, t * LANES : (t + 1) * LANES] = column
            twice[rank + a * ROWS : rank + (a + 1) * ROWS, t * LANES : (t + 1) * LANES] = column
    write_pairs(twice, pairs, rank)
    depth = both.shape[1]
    packed = dot(pairs[:, 0:depth], both[0], 0)
    target = dot(twice[0:rank, 0:depth], both[1], 0)
    for t in range(half // LANES):
        lanes = slice(t * LANES, (t + 1) * LANES)
        unpack(packed[:, lanes], full.at[t], rank)
    for t in range(half // LANES):
        lanes = slice(t * LANES, (t + 1) * LANES)
        out[:, lanes] = solve(full.at[t], target[:, lanes], scaled.at[t], rank)


def place_kernel(own, other, out):
    half = own.shape[1]
    low = pl.multiple_of((lax.axis_index("spec") & 1) * half, LANES)
    out[:, pl.ds(low, half)] = own[...]
    out[:, pl.ds(pl.multiple_of(half - low, LANES), half)] = other[...]


def call(kernel, outs, scratch, *args, space=pltpu.VMEM):
    return pl.pallas_call(
        kernel,
        out_shape=outs,
        in_specs=[pl.BlockSpec(memory_space=space)] * len(args),
        out_specs=jax.tree.map(lambda _: VMEM, outs),
        scratch_shapes=[pltpu.VMEM(s, jnp.float32) if isinstance(s, tuple) else s for s in scratch],
        compiler_params=pltpu.CompilerParams(vmem_limit_bytes=LIMIT),
    )(*args)


def shape(*sizes):
    return jax.ShapeDtypeStruct(sizes, jnp.float32)


def local(peers, groups, spectra_flux, pixel_weights, old_basis):
    spectra, pixels = pixel_weights.shape
    rank = old_basis.shape[0]
    half, chunk = pixels // 2, spectra // groups
    rows = up(chunk, ROWS)
    lead = pair_rows(rank)
    wide = up(lead + rank, LANES)
    inputs = [pltpu.with_memory_space_constraint(a, pltpu.HBM) for a in (spectra_flux, pixel_weights, old_basis)]

    def swap(value, axis, mask):
        return lax.ppermute(value, axis, [(s, s ^ mask) for s in range(peers if axis == "spec" else groups)])

    keep, send, own, other = call(
        functools.partial(spec_kernel, chunk=chunk),
        [shape(groups // 2, rows, wide)] * 2 + [shape(2, spectra, half)] * 2,
        [
            (spectra, pixels),
            (spectra, pixels),
            (rank, pixels),
            (2 * rank, pixels),
            (lead, pixels),
            (groups, rows, wide),
            pltpu.SemaphoreType.DMA((3,)),
        ],
        *inputs,
        space=pl.ANY,
    )
    arrived = swap(send, "pix", 1)
    picks = [own] + [swap(other if q & 1 else own, "spec", q) for q in range(1, peers)]
    sums = call(fold_kernel, [shape(rows, wide)] * (groups // 2), [], keep, arrived)
    parts = [sums[0]] + [swap(sums[k], "pix", 2 * k) for k in range(1, groups // 2)]
    tiles = call(
        functools.partial(coeff_kernel, rank=rank, chunk=chunk),
        shape(peers * groups, ROWS, LANES),
        [(wide, LANES), (rank * rank, LANES), (rank * rank, LANES)],
        *parts,
    )
    tiles = lax.all_to_all(tiles, ("spec", "pix"), 0, 0)
    depth = peers * spectra
    mine = call(
        functools.partial(pixel_kernel, peers=peers, rank=rank, chunk=chunk),
        shape(rank, half),
        [
            (2 * rank, up(depth, LANES)),
            (lead, up(depth, LANES)),
            (2, depth, half),
            (half // LANES, rank * rank, LANES),
            (half // LANES, rank * rank, LANES),
        ],
        tiles,
        *picks,
    )
    return call(place_kernel, shape(rank, pixels), [], mine, swap(mine, "spec", 1))


def solution(mesh):
    placed = (P("spec", "pix"), P("spec", "pix"), P(None, "pix"))
    body = functools.partial(local, mesh.shape["spec"], mesh.shape["pix"])
    return jax.shard_map(body, mesh=mesh, in_specs=placed, out_specs=P(None, "pix"), check_vma=False)
```

```python
import functools

import jax
import jax.numpy as jnp
from jax import lax
from jax.experimental import pallas as pl
from jax.experimental.pallas import tpu as pltpu
from jax.sharding import PartitionSpec as P

LANES = 128
ROWS = 8
VMEM = pl.BlockSpec(memory_space=pltpu.VMEM)
LIMIT = 48 * 1024 * 1024


def up(value, multiple):
    return -(-value // multiple) * multiple


def pair_rows(rank):
    return rank * (rank // 2) + rank // 2


def halves(value):
    high = value.astype(jnp.bfloat16)
    return high, (value - high.astype(jnp.float32)).astype(jnp.bfloat16)


def write_pairs(twice, high, low, rank):
    first = twice[0:rank, :]
    for diag in range(rank // 2 + 1):
        count = rank if diag < rank // 2 else rank // 2
        rows = slice(diag * rank, diag * rank + count)
        high[rows, :], low[rows, :] = halves(first[0:count] * twice[diag : diag + count, :])


def unpack(packed, full, rank):
    for diag in range(rank // 2 + 1):
        base = diag * rank
        count = rank if diag < rank // 2 else rank // 2
        wrap = min(count, rank - diag)
        part = packed[base : base + wrap, :]
        full[pl.ds(diag, wrap, stride=rank + 1), :] = part
        if diag:
            full[pl.ds(diag * rank, wrap, stride=rank + 1), :] = part
        if wrap < count:
            part = packed[base + wrap : base + count, :]
            full[pl.ds(rank - diag, count - wrap, stride=rank + 1), :] = part
            full[pl.ds((rank - diag) * rank, count - wrap, stride=rank + 1), :] = part


def solve(fulls, targets, scaleds, rank):
    row = lax.broadcasted_iota(jnp.int32, targets[0].shape, 0)
    targets, pivots = list(targets), [jnp.zeros_like(target) for target in targets]
    for k in range(rank):
        here = row == k
        for t, (full, scaled) in enumerate(zip(fulls, scaleds)):
            column = full[k * rank : (k + 1) * rank, :]
            for j in range(k):
                column = column - scaled[j * rank : (j + 1) * rank, :] * full[j * rank + k : j * rank + k + 1, :]
            full[k * rank : (k + 1) * rank, :] = column
            factor = jnp.where(here, 0.0, column * (1.0 / column[k : k + 1, :]))
            scaled[k * rank : (k + 1) * rank, :] = factor
            pivots[t] = jnp.where(here, column, pivots[t])
            targets[t] = targets[t] - factor * targets[t][k : k + 1, :]
    return [target / pivot for target, pivot in zip(targets, pivots)]


def dot(left, right, right_axis):
    return lax.dot_general(
        left, right, (((1,), (right_axis,)), ((), ())), preferred_element_type=jnp.float32
    )


def layout(rank, chunk):
    rows = up(chunk, ROWS)
    whole, rest = divmod(pair_rows(rank) + rank, LANES)
    beside = LANES // rest if rest else 1
    tail = -(-(rows // ROWS) // beside) if rest else 0
    return rows, whole, rest, beside, rows * whole + ROWS * tail


def spec_kernel(flux_hbm, weights_hbm, basis_hbm, keep, send, own, other, *scratch, chunk):
    flux, weights, basis, twice, high, low, both, terms, last, grams, sems = scratch
    copies = [
        pltpu.make_async_copy(source, target, sems.at[k])
        for k, (source, target) in enumerate(((basis_hbm, basis), (weights_hbm, weights), (flux_hbm, flux)))
    ]
    for copy in copies:
        copy.start()
    rank, pixels = basis.shape
    spectra = weights.shape[0]
    half = own.shape[2]
    lead = pair_rows(rank)
    copies[0].wait()
    twice[0:rank, :] = basis[...]
    twice[rank:, :] = basis[...]
    terms[0:rank, :], terms[rank:, :] = halves(basis[...])
    write_pairs(twice, high, low, rank)
    copies[1].wait()
    both[0:spectra, :], both[spectra:, :] = halves(weights[...])
    part = dot(both[...], high[...], 1)
    packed = part[spectra:] + dot(both[0:spectra, :], low[...], 1) + part[0:spectra]
    copies[2].wait()
    flux[...] = weights[...] * flux[...]
    both[0:spectra, :], both[spectra:, :] = halves(flux[...])
    part = dot(both[...], terms[...], 1)
    target = part[spectra:, 0:rank] + part[0:spectra, rank:] + part[0:spectra, 0:rank]
    rows, whole, rest, beside, _ = layout(rank, chunk)
    last[:, 0 : rest - rank] = packed[:, lead + rank - rest :]
    last[:, rest - rank : rest] = target
    for k in range(grams.shape[0]):
        for t in range(whole):
            grams[k, t * rows : t * rows + chunk, :] = packed[k * chunk : (k + 1) * chunk, t * LANES : (t + 1) * LANES]
        for g in range(rows // ROWS):
            base, count = rows * whole + g // beside * ROWS, min(ROWS, chunk - g * ROWS)
            lanes = slice(g % beside * rest, (g % beside + 1) * rest)
            grams[k, base : base + count, lanes] = last[k * chunk + g * ROWS : k * chunk + g * ROWS + count, 0:rest]
    for k in range(grams.shape[0] // 2):
        keep[k] = grams[lax.axis_index("pix") ^ (2 * k)]
        send[k] = grams[lax.axis_index("pix") ^ (2 * k + 1)]
    near = pl.multiple_of((lax.axis_index("spec") & 1) * half, LANES)
    far = pl.multiple_of(half - near, LANES)
    own[0] = weights[:, pl.ds(near, half)]
    own[1] = flux[:, pl.ds(near, half)]
    other[0] = weights[:, pl.ds(far, half)]
    other[1] = flux[:, pl.ds(far, half)]


def fold_kernel(keep, arrived, *outs):
    for k, out in enumerate(outs):
        out[...] = keep[k] + arrived[k]


def coeff_kernel(*refs, rank, chunk):
    parts, (out, packed, full, scaled) = refs[:-4], refs[-4:]
    total = parts[0][...]
    for part in parts[1:]:
        total = total + part[...]
    rows, whole, rest, beside, _ = layout(rank, chunk)
    filler = jnp.ones((LANES - rows, LANES), jnp.float32)
    blocks = [total[k * rows : (k + 1) * rows] for k in range(whole)]
    groups = []
    for g in range(rows // ROWS):
        base = rows * whole + g // beside * ROWS
        group = total[base : base + ROWS]
        groups.append(pltpu.roll(group, LANES - g % beside * rest, 1) if g % beside else group)
    blocks.append(jnp.concatenate(groups, axis=0))
    for k, block in enumerate(blocks):
        packed[k * LANES : (k + 1) * LANES, :] = jnp.concatenate([block, filler], axis=0).T
    lead = pair_rows(rank)
    unpack(packed, full, rank)
    (solved,) = solve([full], [packed[lead : lead + rank, :]], [scaled], rank)
    lane = lax.broadcasted_iota(jnp.int32, (ROWS, LANES), 1)
    tile = jnp.zeros((ROWS, LANES), jnp.float32)
    for a in range(rank // ROWS):
        part = solved[a * ROWS : (a + 1) * ROWS, :]
        if a:
            part = pltpu.roll(part, a * chunk, 1)
        tile = jnp.where((lane >= a * chunk) & (lane < (a + 1) * chunk), part, tile)
    for k in range(out.shape[0]):
        out[k] = tile


def pixel_kernel(tiles, *rest, peers, rank, chunk):
    picks, (out, twice, pairs, high, low, full, scaled) = rest[:peers], rest[peers:]
    spectra = picks[0].shape[1]
    half = picks[0].shape[2]
    group = spectra // chunk
    lane = lax.broadcasted_iota(jnp.int32, (ROWS, LANES), 1)
    width = twice.shape[1]
    for q in range(peers):
        rows = slice(q * spectra, (q + 1) * spectra)
        for k in range(2):
            high[k, rows, :], low[k, rows, :] = halves(picks[q][k])
    for a in range(rank // ROWS):
        columns = [jnp.zeros((ROWS, LANES), jnp.float32) for _ in range(width // LANES)]
        for q in range(peers):
            for k in range(group):
                part = tiles[(lax.axis_index("spec") ^ q) * group + k]
                start = q * spectra + k * chunk
                shift = (start - a * chunk) % LANES
                if shift:
                    part = pltpu.roll(part, shift, 1)
                for t in range(start // LANES, (start + chunk - 1) // LANES + 1):
                    begin, end = max(start - t * LANES, 0), min(start + chunk - t * LANES, LANES)
                    columns[t] = jnp.where((lane >= begin) & (lane < end), part, columns[t])
        for t, column in enumerate(columns):
            twice[a * ROWS : (a + 1) * ROWS, t * LANES : (t + 1) * LANES] = column
            twice[rank + a * ROWS : rank + (a + 1) * ROWS, t * LANES : (t + 1) * LANES] = column
    depth = high.shape[1]
    lead = pair_rows(rank)
    write_pairs(twice, pairs.at[0:lead], pairs.at[lead : 2 * lead], rank)
    part = dot(pairs[:, 0:depth], high[0], 0)
    packed = part[lead:] + dot(pairs[0:lead, 0:depth], low[0], 0) + part[0:lead]
    terms = jnp.concatenate(halves(twice[0:rank, 0:depth]), axis=0)
    part = dot(terms, high[1], 0)
    target = part[rank:] + dot(terms[0:rank], low[1], 0) + part[0:rank]
    tiles = range(half // LANES)
    for t in tiles:
        unpack(packed[:, t * LANES : (t + 1) * LANES], full.at[t], rank)
    solved = solve(
        [full.at[t] for t in tiles],
        [target[:, t * LANES : (t + 1) * LANES] for t in tiles],
        [scaled.at[t] for t in tiles],
        rank,
    )
    for t in tiles:
        out[:, t * LANES : (t + 1) * LANES] = solved[t]


def place_kernel(own, other, out):
    half = own.shape[1]
    low = pl.multiple_of((lax.axis_index("spec") & 1) * half, LANES)
    out[:, pl.ds(low, half)] = own[...]
    out[:, pl.ds(pl.multiple_of(half - low, LANES), half)] = other[...]


def scratch_shape(sizes):
    if not isinstance(sizes, tuple):
        return sizes
    if sizes[0] is jnp.bfloat16:
        return pltpu.VMEM(sizes[1:], jnp.bfloat16)
    return pltpu.VMEM(sizes, jnp.float32)


def call(kernel, outs, scratch, *args, space=pltpu.VMEM):
    return pl.pallas_call(
        kernel,
        out_shape=outs,
        in_specs=[pl.BlockSpec(memory_space=space)] * len(args),
        out_specs=jax.tree.map(lambda _: VMEM, outs),
        scratch_shapes=[scratch_shape(s) for s in scratch],
        compiler_params=pltpu.CompilerParams(vmem_limit_bytes=LIMIT),
    )(*args)


def shape(*sizes):
    return jax.ShapeDtypeStruct(sizes, jnp.float32)


def local(peers, groups, spectra_flux, pixel_weights, old_basis):
    spectra, pixels = pixel_weights.shape
    rank = old_basis.shape[0]
    half, chunk = pixels // 2, spectra // groups
    lead = pair_rows(rank)
    wide = up(lead + rank, LANES)
    rows = layout(rank, chunk)[-1]
    half_type = jnp.bfloat16
    inputs = [pltpu.with_memory_space_constraint(a, pltpu.HBM) for a in (spectra_flux, pixel_weights, old_basis)]

    def swap(value, axis, mask):
        return lax.ppermute(value, axis, [(s, s ^ mask) for s in range(peers if axis == "spec" else groups)])

    keep, send, own, other = call(
        functools.partial(spec_kernel, chunk=chunk),
        [shape(groups // 2, rows, LANES)] * 2 + [shape(2, spectra, half)] * 2,
        [
            (spectra, pixels),
            (spectra, pixels),
            (rank, pixels),
            (2 * rank, pixels),
            (half_type, lead, pixels),
            (half_type, lead, pixels),
            (half_type, 2 * spectra, pixels),
            (half_type, 2 * rank, pixels),
            (spectra, LANES),
            (groups, rows, LANES),
            pltpu.SemaphoreType.DMA((3,)),
        ],
        *inputs,
        space=pl.ANY,
    )
    arrived = swap(send, "pix", 1)
    picks = [own] + [swap(other if q & 1 else own, "spec", q) for q in range(1, peers)]
    sums = call(fold_kernel, [shape(rows, LANES)] * (groups // 2), [], keep, arrived)
    parts = [sums[0]] + [swap(sums[k], "pix", 2 * k) for k in range(1, groups // 2)]
    tiles = call(
        functools.partial(coeff_kernel, rank=rank, chunk=chunk),
        shape(peers * groups, ROWS, LANES),
        [(wide, LANES), (rank * rank, LANES), (rank * rank, LANES)],
        *parts,
    )
    tiles = lax.all_to_all(tiles, ("spec", "pix"), 0, 0)
    depth = peers * spectra
    mine = call(
        functools.partial(pixel_kernel, peers=peers, rank=rank, chunk=chunk),
        shape(rank, half),
        [
            (2 * rank, up(depth, LANES)),
            (half_type, 2 * lead, up(depth, LANES)),
            (half_type, 2, depth, half),
            (half_type, 2, depth, half),
            (half // LANES, rank * rank, LANES),
            (half // LANES, rank * rank, LANES),
        ],
        tiles,
        *picks,
    )
    return call(place_kernel, shape(rank, pixels), [], mine, swap(mine, "spec", 1))


def solution(mesh):
    placed = (P("spec", "pix"), P("spec", "pix"), P(None, "pix"))
    body = functools.partial(local, mesh.shape["spec"], mesh.shape["pix"])
    return jax.shard_map(body, mesh=mesh, in_specs=placed, out_specs=P(None, "pix"), check_vma=False)
```

```python
import functools

import jax
import jax.numpy as jnp
from jax import lax
from jax.experimental import pallas as pl
from jax.experimental.pallas import tpu as pltpu
from jax.sharding import PartitionSpec as P

LANES = 128
ROWS = 8
VMEM = pl.BlockSpec(memory_space=pltpu.VMEM)
SPAN = 4
LIMIT = 48 * 1024 * 1024


def pixel_place():
    return lax.axis_index("high") * SPAN + lax.axis_index("low")


def up(value, multiple):
    return -(-value // multiple) * multiple


def pair_rows(rank):
    return rank * (rank // 2) + rank // 2


def halves(value):
    high = value.astype(jnp.bfloat16)
    return high, (value - high.astype(jnp.float32)).astype(jnp.bfloat16)


def write_pairs(twice, high, low, rank):
    first = twice[0:rank, :]
    for diag in range(rank // 2 + 1):
        count = rank if diag < rank // 2 else rank // 2
        rows = slice(diag * rank, diag * rank + count)
        high[rows, :], low[rows, :] = halves(first[0:count] * twice[diag : diag + count, :])


def unpack(packed, full, rank):
    for diag in range(rank // 2 + 1):
        base = diag * rank
        count = rank if diag < rank // 2 else rank // 2
        wrap = min(count, rank - diag)
        part = packed[base : base + wrap, :]
        full[pl.ds(diag, wrap, stride=rank + 1), :] = part
        if diag:
            full[pl.ds(diag * rank, wrap, stride=rank + 1), :] = part
        if wrap < count:
            part = packed[base + wrap : base + count, :]
            full[pl.ds(rank - diag, count - wrap, stride=rank + 1), :] = part
            full[pl.ds((rank - diag) * rank, count - wrap, stride=rank + 1), :] = part


def solve(fulls, targets, scaleds, rank):
    row = lax.broadcasted_iota(jnp.int32, targets[0].shape, 0)
    targets, pivots = list(targets), [jnp.zeros_like(target) for target in targets]
    for k in range(rank):
        here = row == k
        for t, (full, scaled) in enumerate(zip(fulls, scaleds)):
            column = full[k * rank : (k + 1) * rank, :]
            for j in range(k):
                column = column - scaled[j * rank : (j + 1) * rank, :] * full[j * rank + k : j * rank + k + 1, :]
            full[k * rank : (k + 1) * rank, :] = column
            factor = jnp.where(here, 0.0, column * (1.0 / column[k : k + 1, :]))
            scaled[k * rank : (k + 1) * rank, :] = factor
            pivots[t] = jnp.where(here, column, pivots[t])
            targets[t] = targets[t] - factor * targets[t][k : k + 1, :]
    return [target / pivot for target, pivot in zip(targets, pivots)]


def dot(left, right, right_axis):
    return lax.dot_general(
        left, right, (((1,), (right_axis,)), ((), ())), preferred_element_type=jnp.float32
    )


def layout(rank, chunk):
    rows = up(chunk, ROWS)
    whole, rest = divmod(pair_rows(rank) + rank, LANES)
    beside = LANES // rest if rest else 1
    tail = -(-(rows // ROWS) // beside) if rest else 0
    return rows, whole, rest, beside, rows * whole + ROWS * tail


def spec_kernel(flux_hbm, weights_hbm, basis_hbm, own, other, *rest, chunk, span):
    sends, scratch = rest[:span], rest[span:]
    flux, weights, basis, twice, high, low, both, terms, last, grams, sems = scratch
    rank, pixels = basis.shape
    spectra = weights.shape[0]
    half = own.shape[2]
    near = pl.multiple_of((lax.axis_index("spec") & 1) * half, LANES)
    far = pl.multiple_of(half - near, LANES)
    moves = [(basis_hbm, basis), (weights_hbm, weights), (flux_hbm, flux)]
    moves += [(flux_hbm.at[:, pl.ds(far, half)], other.at[1]), (weights_hbm.at[:, pl.ds(far, half)], other.at[0])]
    moves += [(flux_hbm.at[:, pl.ds(near, half)], own.at[1]), (weights_hbm.at[:, pl.ds(near, half)], own.at[0])]
    copies = [pltpu.make_async_copy(source, target, sems.at[k]) for k, (source, target) in enumerate(moves)]
    for copy in copies:
        copy.start()
    lead = pair_rows(rank)
    copies[0].wait()
    twice[0:rank, :] = basis[...]
    twice[rank:, :] = basis[...]
    terms[0:rank, :], terms[rank:, :] = halves(basis[...])
    write_pairs(twice, high, low, rank)
    copies[1].wait()
    both[0:spectra, :], both[spectra:, :] = halves(weights[...])
    part = dot(both[...], high[...], 1)
    packed = part[spectra:] + dot(both[0:spectra, :], low[...], 1) + part[0:spectra]
    copies[2].wait()
    flux[...] = weights[...] * flux[...]
    both[0:spectra, :], both[spectra:, :] = halves(flux[...])
    part = dot(both[...], terms[...], 1)
    target = part[spectra:, 0:rank] + part[0:spectra, rank:] + part[0:spectra, 0:rank]
    rows, whole, rest, beside, _ = layout(rank, chunk)
    last[:, 0 : rest - rank] = packed[:, lead + rank - rest :]
    last[:, rest - rank : rest] = target
    for k in range(grams.shape[0]):
        for t in range(whole):
            grams[k, t * rows : t * rows + chunk, :] = packed[k * chunk : (k + 1) * chunk, t * LANES : (t + 1) * LANES]
        for g in range(rows // ROWS):
            base, count = rows * whole + g // beside * ROWS, min(ROWS, chunk - g * ROWS)
            lanes = slice(g % beside * rest, (g % beside + 1) * rest)
            grams[k, base : base + count, lanes] = last[k * chunk + g * ROWS : k * chunk + g * ROWS + count, 0:rest]
    for k in range(grams.shape[0] // span):
        for m, send in enumerate(sends):
            send[k] = grams[pixel_place() ^ (span * k + m)]
    for copy in copies[3:]:
        copy.wait()


def add_kernel(*refs, flip):
    for h in range(refs[0].shape[0]):
        total = refs[0][h]
        for term in refs[1:-1]:
            total = total + term[h ^ flip]
        refs[-1][h] = total


def coeff_kernel(sums, arrived, out, packed, full, scaled, *, rank, chunk):
    chunks = sums.shape[0]
    total = [sums[h] + arrived[h ^ (chunks // 2)] for h in range(chunks)]
    rows, whole, rest, beside, _ = layout(rank, chunk)
    filler = jnp.ones((LANES - chunks * rows, LANES), jnp.float32)
    for t in range(whole):
        block = [total[h][t * rows : (t + 1) * rows] for h in range(chunks)]
        packed[t * LANES : (t + 1) * LANES, :] = jnp.concatenate(block + [filler], axis=0).T
    groups = []
    for h in range(chunks):
        for g in range(rows // ROWS):
            base = rows * whole + g // beside * ROWS
            group = total[h][base : base + ROWS]
            groups.append(pltpu.roll(group, LANES - g % beside * rest, 1) if g % beside else group)
    packed[whole * LANES :, :] = jnp.concatenate(groups + [filler], axis=0).T
    lead = pair_rows(rank)
    unpack(packed, full, rank)
    (solved,) = solve([full], [packed[lead : lead + rank, :]], [scaled], rank)
    lane = lax.broadcasted_iota(jnp.int32, (ROWS, LANES), 1)
    for h in range(chunks):
        tile = jnp.zeros((ROWS, LANES), jnp.float32)
        for a in range(rank // ROWS):
            part = solved[a * ROWS : (a + 1) * ROWS, :]
            shift = (a * chunk - h * rows) % LANES
            if shift:
                part = pltpu.roll(part, shift, 1)
            tile = jnp.where((lane >= a * chunk) & (lane < (a + 1) * chunk), part, tile)
        for k in range(out.shape[0]):
            out[k, h] = tile


def terms_kernel(*refs, peers):
    picks, (high, low) = refs[:peers], refs[peers:]
    spectra = picks[0].shape[1]
    for q, pick in enumerate(picks):
        rows = pl.ds(pl.multiple_of((lax.axis_index("spec") ^ q) * spectra, 16), spectra)
        high[0, rows, :], low[0, rows, :] = halves(pick[0])
        high[1, rows, :], low[1, rows, :] = halves(pick[0] * pick[1])


def pixel_kernel(tiles, high, low, out, twice, pairs, full, scaled, *, peers, rank, chunk):
    spectra = high.shape[1] // peers
    half = high.shape[2]
    group = spectra // chunk
    lane = lax.broadcasted_iota(jnp.int32, (ROWS, LANES), 1)
    width = twice.shape[1]
    for a in range(rank // ROWS):
        columns = [jnp.zeros((ROWS, LANES), jnp.float32) for _ in range(width // LANES)]
        for q in range(peers):
            for k in range(group):
                near = pixel_place() ^ k
                part = tiles[q * SPAN + k % SPAN, near // SPAN]
                start = q * spectra + k * chunk
                shift = (start - a * chunk) % LANES
                if shift:
                    part = pltpu.roll(part, shift, 1)
                for t in range(start // LANES, (start + chunk - 1) // LANES + 1):
                    begin, end = max(start - t * LANES, 0), min(start + chunk - t * LANES, LANES)
                    columns[t] = jnp.where((lane >= begin) & (lane < end), part, columns[t])
        for t, column in enumerate(columns):
            twice[a * ROWS : (a + 1) * ROWS, t * LANES : (t + 1) * LANES] = column
            twice[rank + a * ROWS : rank + (a + 1) * ROWS, t * LANES : (t + 1) * LANES] = column
    depth = high.shape[1]
    lead = pair_rows(rank)
    write_pairs(twice, pairs.at[0:lead], pairs.at[lead : 2 * lead], rank)
    part = dot(pairs[:, 0:depth], high[0], 0)
    packed = part[lead:] + dot(pairs[0:lead, 0:depth], low[0], 0) + part[0:lead]
    terms = jnp.concatenate(halves(twice[0:rank, 0:depth]), axis=0)
    part = dot(terms, high[1], 0)
    target = part[rank:] + dot(terms[0:rank], low[1], 0) + part[0:rank]
    tiles = range(half // LANES)
    for t in tiles:
        unpack(packed[:, t * LANES : (t + 1) * LANES], full.at[t], rank)
    solved = solve(
        [full.at[t] for t in tiles],
        [target[:, t * LANES : (t + 1) * LANES] for t in tiles],
        [scaled.at[t] for t in tiles],
        rank,
    )
    for t in tiles:
        out[:, t * LANES : (t + 1) * LANES] = solved[t]


def place_kernel(own, other, out):
    half = own.shape[1]
    low = pl.multiple_of((lax.axis_index("spec") & 1) * half, LANES)
    out[:, pl.ds(low, half)] = own[...]
    out[:, pl.ds(pl.multiple_of(half - low, LANES), half)] = other[...]


def scratch_shape(sizes):
    if not isinstance(sizes, tuple):
        return sizes
    if sizes[0] is jnp.bfloat16:
        return pltpu.VMEM(sizes[1:], jnp.bfloat16)
    return pltpu.VMEM(sizes, jnp.float32)


def call(kernel, outs, scratch, *args, space=pltpu.VMEM):
    return pl.pallas_call(
        kernel,
        out_shape=outs,
        in_specs=[pl.BlockSpec(memory_space=space)] * len(args),
        out_specs=jax.tree.map(lambda _: VMEM, outs),
        scratch_shapes=[scratch_shape(s) for s in scratch],
        compiler_params=pltpu.CompilerParams(vmem_limit_bytes=LIMIT),
    )(*args)


def shape(*sizes):
    return jax.ShapeDtypeStruct(sizes, jnp.float32)


def local(peers, groups, spectra_flux, pixel_weights, old_basis):
    spectra, pixels = pixel_weights.shape
    rank = old_basis.shape[0]
    half, chunk = pixels // 2, spectra // groups
    lead = pair_rows(rank)
    wide = up(lead + rank, LANES)
    rows = layout(rank, chunk)[-1]
    half_type = jnp.bfloat16
    inputs = [pltpu.with_memory_space_constraint(a, pltpu.HBM) for a in (spectra_flux, pixel_weights, old_basis)]

    def swap(value, axis, mask):
        axis, size = ("spec", peers) if axis == "spec" else (("high", "low"), groups)
        return lax.ppermute(value, axis, [(s, s ^ mask) for s in range(size)])

    own, other, *sends = call(
        functools.partial(spec_kernel, chunk=chunk, span=SPAN),
        [shape(2, spectra, half)] * 2 + [shape(groups // SPAN, rows, LANES)] * SPAN,
        [
            (spectra, pixels),
            (spectra, pixels),
            (rank, pixels),
            (2 * rank, pixels),
            (half_type, lead, pixels),
            (half_type, lead, pixels),
            (half_type, 2 * spectra, pixels),
            (half_type, 2 * rank, pixels),
            (spectra, LANES),
            (groups, rows, LANES),
            pltpu.SemaphoreType.DMA((7,)),
        ],
        *inputs,
        space=pl.ANY,
    )
    arrived = [swap(sends[m], "pix", m) for m in range(SPAN - 1, 0, -1)]
    picks = [own] + [swap(other if q & 1 else own, "spec", q) for q in range(1, peers)]
    kept = shape(*sends[0].shape)
    sums = call(functools.partial(add_kernel, flip=0), kept, [], sends[0], *arrived)
    reach = SPAN
    while 2 * reach < groups:
        sums = call(functools.partial(add_kernel, flip=reach // SPAN), kept, [], sums, swap(sums, "pix", reach))
        reach *= 2
    tiles = call(
        functools.partial(coeff_kernel, rank=rank, chunk=chunk),
        shape(peers * SPAN, groups // SPAN, ROWS, LANES),
        [(wide, LANES), (rank * rank, LANES), (rank * rank, LANES)],
        sums,
        swap(sums, "pix", reach),
    )
    tiles = lax.all_to_all(tiles, ("spec", "low"), 0, 0)
    depth = peers * spectra
    terms = [jax.ShapeDtypeStruct((2, depth, half), jnp.bfloat16)] * 2
    high, low = call(functools.partial(terms_kernel, peers=peers), terms, [], *picks)
    mine = call(
        functools.partial(pixel_kernel, peers=peers, rank=rank, chunk=chunk),
        shape(rank, half),
        [
            (2 * rank, up(depth, LANES)),
            (half_type, 2 * lead, up(depth, LANES)),
            (half // LANES, rank * rank, LANES),
            (half // LANES, rank * rank, LANES),
        ],
        tiles,
        high,
        low,
    )
    return call(place_kernel, shape(rank, pixels), [], mine, swap(mine, "spec", 1))


def solution(mesh):
    peers, groups = mesh.shape["spec"], mesh.shape["pix"]
    split = jax.sharding.Mesh(mesh.devices.reshape(peers, groups // SPAN, SPAN), ("spec", "high", "low"))
    pix = ("high", "low")
    body = functools.partial(local, peers, groups)
    placed = (P("spec", pix), P("spec", pix), P(None, pix))
    return jax.shard_map(body, mesh=split, in_specs=placed, out_specs=P(None, pix), check_vma=False)
```

```python
import functools

import jax
import jax.numpy as jnp
from jax import lax
from jax.experimental import pallas as pl
from jax.experimental.pallas import tpu as pltpu
from jax.sharding import PartitionSpec as P

LANES = 128
ROWS = 8
VMEM = pl.BlockSpec(memory_space=pltpu.VMEM)
SPAN = 4
LIMIT = 48 * 1024 * 1024


def pixel_place():
    return lax.axis_index("high") * SPAN + lax.axis_index("low")


def up(value, multiple):
    return -(-value // multiple) * multiple


def pair_rows(rank):
    return rank * (rank // 2) + rank // 2


def halves(value):
    high = value.astype(jnp.bfloat16)
    return high, (value - high.astype(jnp.float32)).astype(jnp.bfloat16)


def write_pairs(twice, high, low, rank):
    first = twice[0:rank, :]
    for diag in range(rank // 2 + 1):
        count = rank if diag < rank // 2 else rank // 2
        rows = slice(diag * rank, diag * rank + count)
        high[rows, :], low[rows, :] = halves(first[0:count] * twice[diag : diag + count, :])


def unpack(packed, full, rank):
    for diag in range(rank // 2 + 1):
        base = diag * rank
        count = rank if diag < rank // 2 else rank // 2
        wrap = min(count, rank - diag)
        part = packed[base : base + wrap, :]
        full[pl.ds(diag, wrap, stride=rank + 1), :] = part
        if diag:
            full[pl.ds(diag * rank, wrap, stride=rank + 1), :] = part
        if wrap < count:
            part = packed[base + wrap : base + count, :]
            full[pl.ds(rank - diag, count - wrap, stride=rank + 1), :] = part
            full[pl.ds((rank - diag) * rank, count - wrap, stride=rank + 1), :] = part


def solve(fulls, targets, scaleds, rank):
    row = lax.broadcasted_iota(jnp.int32, (ROWS, LANES), 0)
    blocks = rank // ROWS
    targets = [[target[b * ROWS : (b + 1) * ROWS, :] for b in range(blocks)] for target in targets]
    pivots = [[jnp.zeros((ROWS, LANES), jnp.float32) for _ in range(blocks)] for _ in targets]
    tiles = range(len(targets))

    def part(k, b):
        return slice(k * rank + b * ROWS, k * rank + (b + 1) * ROWS)

    def reduced(t, k, b, stop):
        value = fulls[t][part(k, b), :]
        for j in range(stop):
            value = value - scaleds[t][part(j, b), :] * fulls[t][j * rank + k : j * rank + k + 1, :]
        return value

    for k in range(rank):
        first, place = k // ROWS, k % ROWS
        here = row == place
        for t in tiles:
            column = [reduced(t, k, b, k) for b in range(first, blocks)]
            inverse = 1.0 / column[0][place : place + 1, :]
            pivots[t][first] = jnp.where(here, column[0], pivots[t][first])
            known = targets[t][first][place : place + 1, :]
            for b in range(first, blocks):
                fulls[t][part(k, b), :] = column[b - first]
                factor = column[b - first] * inverse
                if b == first:
                    factor = jnp.where(here, 0.0, factor)
                scaleds[t][part(k, b), :] = factor
                targets[t][b] = targets[t][b] - factor * known
        if place == ROWS - 1:
            for t in tiles:
                for later in range(k + 1, rank):
                    fulls[t][part(later, first), :] = reduced(t, later, first, k + 1)
    for b in reversed(range(blocks)):
        for t in tiles:
            for k in reversed(range((b + 1) * ROWS, rank)):
                known = targets[t][k // ROWS][k % ROWS : k % ROWS + 1, :]
                targets[t][b] = targets[t][b] - fulls[t][part(k, b), :] * known
            targets[t][b] = targets[t][b] / pivots[t][b]
    return [jnp.concatenate(target, axis=0) for target in targets]


def dot(left, right, right_axis):
    return lax.dot_general(
        left, right, (((1,), (right_axis,)), ((), ())), preferred_element_type=jnp.float32
    )


def layout(rank, chunk):
    rows = up(chunk, ROWS)
    whole, rest = divmod(pair_rows(rank) + rank, LANES)
    beside = LANES // rest if rest else 1
    tail = -(-(rows // ROWS) // beside) if rest else 0
    return rows, whole, rest, beside, rows * whole + ROWS * tail


def spec_kernel(flux_hbm, weights_hbm, basis_hbm, own, other, *rest, chunk, span):
    sends, scratch = rest[:span], rest[span:]
    flux, weights, basis, twice, high, low, both, terms, last, grams, sems = scratch
    rank, pixels = basis.shape
    spectra = weights.shape[0]
    half = own.shape[2]
    near = pl.multiple_of((lax.axis_index("spec") & 1) * half, LANES)
    far = pl.multiple_of(half - near, LANES)
    moves = [(basis_hbm, basis), (weights_hbm, weights), (flux_hbm, flux)]
    moves += [(flux_hbm.at[:, pl.ds(far, half)], other.at[1]), (weights_hbm.at[:, pl.ds(far, half)], other.at[0])]
    moves += [(flux_hbm.at[:, pl.ds(near, half)], own.at[1]), (weights_hbm.at[:, pl.ds(near, half)], own.at[0])]
    copies = [pltpu.make_async_copy(source, target, sems.at[k]) for k, (source, target) in enumerate(moves)]
    for copy in copies:
        copy.start()
    lead = pair_rows(rank)
    copies[0].wait()
    twice[0:rank, :] = basis[...]
    twice[rank:, :] = basis[...]
    terms[0:rank, :], terms[rank:, :] = halves(basis[...])
    write_pairs(twice, high, low, rank)
    copies[1].wait()
    both[0:spectra, :], both[spectra:, :] = halves(weights[...])
    part = dot(both[...], high[...], 1)
    packed = part[spectra:] + dot(both[0:spectra, :], low[...], 1) + part[0:spectra]
    copies[2].wait()
    flux[...] = weights[...] * flux[...]
    both[0:spectra, :], both[spectra:, :] = halves(flux[...])
    part = dot(both[...], terms[...], 1)
    target = part[spectra:, 0:rank] + part[0:spectra, rank:] + part[0:spectra, 0:rank]
    rows, whole, rest, beside, _ = layout(rank, chunk)
    last[:, 0 : rest - rank] = packed[:, lead + rank - rest :]
    last[:, rest - rank : rest] = target
    for k in range(grams.shape[0]):
        for t in range(whole):
            grams[k, t * rows : t * rows + chunk, :] = packed[k * chunk : (k + 1) * chunk, t * LANES : (t + 1) * LANES]
        for g in range(rows // ROWS):
            base, count = rows * whole + g // beside * ROWS, min(ROWS, chunk - g * ROWS)
            lanes = slice(g % beside * rest, (g % beside + 1) * rest)
            grams[k, base : base + count, lanes] = last[k * chunk + g * ROWS : k * chunk + g * ROWS + count, 0:rest]
    for k in range(grams.shape[0] // span):
        for m, send in enumerate(sends):
            send[k] = grams[pixel_place() ^ (span * k + m)]
    for copy in copies[3:]:
        copy.wait()


def add_kernel(*refs, flip):
    for h in range(refs[0].shape[0]):
        total = refs[0][h]
        for term in refs[1:-1]:
            total = total + term[h ^ flip]
        refs[-1][h] = total


def coeff_kernel(sums, arrived, out, packed, full, scaled, *, rank, chunk):
    chunks = sums.shape[0]
    total = [sums[h] + arrived[h ^ (chunks // 2)] for h in range(chunks)]
    rows, whole, rest, beside, _ = layout(rank, chunk)
    filler = jnp.ones((LANES - chunks * rows, LANES), jnp.float32)
    for t in range(whole):
        block = [total[h][t * rows : (t + 1) * rows] for h in range(chunks)]
        packed[t * LANES : (t + 1) * LANES, :] = jnp.concatenate(block + [filler], axis=0).T
    groups = []
    for h in range(chunks):
        for g in range(rows // ROWS):
            base = rows * whole + g // beside * ROWS
            group = total[h][base : base + ROWS]
            groups.append(pltpu.roll(group, LANES - g % beside * rest, 1) if g % beside else group)
    packed[whole * LANES :, :] = jnp.concatenate(groups + [filler], axis=0).T
    lead = pair_rows(rank)
    unpack(packed, full, rank)
    (solved,) = solve([full], [packed[lead : lead + rank, :]], [scaled], rank)
    lane = lax.broadcasted_iota(jnp.int32, (ROWS, LANES), 1)
    for h in range(chunks):
        tile = jnp.zeros((ROWS, LANES), jnp.float32)
        for a in range(rank // ROWS):
            part = solved[a * ROWS : (a + 1) * ROWS, :]
            shift = (a * chunk - h * rows) % LANES
            if shift:
                part = pltpu.roll(part, shift, 1)
            tile = jnp.where((lane >= a * chunk) & (lane < (a + 1) * chunk), part, tile)
        for k in range(out.shape[0]):
            out[k, h] = tile


def terms_kernel(*refs, peers):
    picks, (high, low) = refs[:peers], refs[peers:]
    spectra = picks[0].shape[1]
    for q, pick in enumerate(picks):
        rows = pl.ds(pl.multiple_of((lax.axis_index("spec") ^ q) * spectra, 16), spectra)
        high[0, rows, :], low[0, rows, :] = halves(pick[0])
        high[1, rows, :], low[1, rows, :] = halves(pick[0] * pick[1])


def pixel_kernel(tiles, high, low, out, twice, pairs, full, scaled, *, peers, rank, chunk):
    spectra = high.shape[1] // peers
    half = high.shape[2]
    group = spectra // chunk
    lane = lax.broadcasted_iota(jnp.int32, (ROWS, LANES), 1)
    width = twice.shape[1]
    for a in range(rank // ROWS):
        columns = [jnp.zeros((ROWS, LANES), jnp.float32) for _ in range(width // LANES)]
        for q in range(peers):
            for k in range(group):
                near = pixel_place() ^ k
                part = tiles[q * SPAN + k % SPAN, near // SPAN]
                start = q * spectra + k * chunk
                shift = (start - a * chunk) % LANES
                if shift:
                    part = pltpu.roll(part, shift, 1)
                for t in range(start // LANES, (start + chunk - 1) // LANES + 1):
                    begin, end = max(start - t * LANES, 0), min(start + chunk - t * LANES, LANES)
                    columns[t] = jnp.where((lane >= begin) & (lane < end), part, columns[t])
        for t, column in enumerate(columns):
            twice[a * ROWS : (a + 1) * ROWS, t * LANES : (t + 1) * LANES] = column
            twice[rank + a * ROWS : rank + (a + 1) * ROWS, t * LANES : (t + 1) * LANES] = column
    depth = high.shape[1]
    lead = pair_rows(rank)
    write_pairs(twice, pairs.at[0:lead], pairs.at[lead : 2 * lead], rank)
    part = dot(pairs[:, 0:depth], high[0], 0)
    packed = part[lead:] + dot(pairs[0:lead, 0:depth], low[0], 0) + part[0:lead]
    terms = jnp.concatenate(halves(twice[0:rank, 0:depth]), axis=0)
    part = dot(terms, high[1], 0)
    target = part[rank:] + dot(terms[0:rank], low[1], 0) + part[0:rank]
    tiles = range(half // LANES)
    for t in tiles:
        unpack(packed[:, t * LANES : (t + 1) * LANES], full.at[t], rank)
    solved = solve(
        [full.at[t] for t in tiles],
        [target[:, t * LANES : (t + 1) * LANES] for t in tiles],
        [scaled.at[t] for t in tiles],
        rank,
    )
    for t in tiles:
        out[:, t * LANES : (t + 1) * LANES] = solved[t]


def place_kernel(own, other, out):
    half = own.shape[1]
    low = pl.multiple_of((lax.axis_index("spec") & 1) * half, LANES)
    out[:, pl.ds(low, half)] = own[...]
    out[:, pl.ds(pl.multiple_of(half - low, LANES), half)] = other[...]


def scratch_shape(sizes):
    if not isinstance(sizes, tuple):
        return sizes
    if sizes[0] is jnp.bfloat16:
        return pltpu.VMEM(sizes[1:], jnp.bfloat16)
    return pltpu.VMEM(sizes, jnp.float32)


def call(kernel, outs, scratch, *args, space=pltpu.VMEM):
    return pl.pallas_call(
        kernel,
        out_shape=outs,
        in_specs=[pl.BlockSpec(memory_space=space)] * len(args),
        out_specs=jax.tree.map(lambda _: VMEM, outs),
        scratch_shapes=[scratch_shape(s) for s in scratch],
        compiler_params=pltpu.CompilerParams(vmem_limit_bytes=LIMIT),
    )(*args)


def shape(*sizes):
    return jax.ShapeDtypeStruct(sizes, jnp.float32)


def local(peers, groups, spectra_flux, pixel_weights, old_basis):
    spectra, pixels = pixel_weights.shape
    rank = old_basis.shape[0]
    half, chunk = pixels // 2, spectra // groups
    lead = pair_rows(rank)
    wide = up(lead + rank, LANES)
    rows = layout(rank, chunk)[-1]
    half_type = jnp.bfloat16
    inputs = [pltpu.with_memory_space_constraint(a, pltpu.HBM) for a in (spectra_flux, pixel_weights, old_basis)]

    def swap(value, axis, mask):
        axis, size = ("spec", peers) if axis == "spec" else (("high", "low"), groups)
        return lax.ppermute(value, axis, [(s, s ^ mask) for s in range(size)])

    own, other, *sends = call(
        functools.partial(spec_kernel, chunk=chunk, span=SPAN),
        [shape(2, spectra, half)] * 2 + [shape(groups // SPAN, rows, LANES)] * SPAN,
        [
            (spectra, pixels),
            (spectra, pixels),
            (rank, pixels),
            (2 * rank, pixels),
            (half_type, lead, pixels),
            (half_type, lead, pixels),
            (half_type, 2 * spectra, pixels),
            (half_type, 2 * rank, pixels),
            (spectra, LANES),
            (groups, rows, LANES),
            pltpu.SemaphoreType.DMA((7,)),
        ],
        *inputs,
        space=pl.ANY,
    )
    arrived = [swap(sends[m], "pix", m) for m in range(SPAN - 1, 0, -1)]
    picks = [own] + [swap(other if q & 1 else own, "spec", q) for q in range(1, peers)]
    kept = shape(*sends[0].shape)
    sums = call(functools.partial(add_kernel, flip=0), kept, [], sends[0], *arrived)
    reach = SPAN
    while 2 * reach < groups:
        sums = call(functools.partial(add_kernel, flip=reach // SPAN), kept, [], sums, swap(sums, "pix", reach))
        reach *= 2
    tiles = call(
        functools.partial(coeff_kernel, rank=rank, chunk=chunk),
        shape(peers * SPAN, groups // SPAN, ROWS, LANES),
        [(wide, LANES), (rank * rank, LANES), (rank * rank, LANES)],
        sums,
        swap(sums, "pix", reach),
    )
    tiles = lax.all_to_all(tiles, ("spec", "low"), 0, 0)
    depth = peers * spectra
    terms = [jax.ShapeDtypeStruct((2, depth, half), jnp.bfloat16)] * 2
    high, low = call(functools.partial(terms_kernel, peers=peers), terms, [], *picks)
    mine = call(
        functools.partial(pixel_kernel, peers=peers, rank=rank, chunk=chunk),
        shape(rank, half),
        [
            (2 * rank, up(depth, LANES)),
            (half_type, 2 * lead, up(depth, LANES)),
            (half // LANES, rank * rank, LANES),
            (half // LANES, rank * rank, LANES),
        ],
        tiles,
        high,
        low,
    )
    return call(place_kernel, shape(rank, pixels), [], mine, swap(mine, "spec", 1))


def solution(mesh):
    peers, groups = mesh.shape["spec"], mesh.shape["pix"]
    split = jax.sharding.Mesh(mesh.devices.reshape(peers, groups // SPAN, SPAN), ("spec", "high", "low"))
    pix = ("high", "low")
    body = functools.partial(local, peers, groups)
    placed = (P("spec", pix), P("spec", pix), P(None, pix))
    return jax.shard_map(body, mesh=split, in_specs=placed, out_specs=P(None, pix), check_vma=False)
```

```python
import functools

import jax
import jax.numpy as jnp
from jax import lax
from jax.experimental import pallas as pl
from jax.experimental.pallas import tpu as pltpu
from jax.sharding import PartitionSpec as P

LANES = 128
ROWS = 8
VMEM = pl.BlockSpec(memory_space=pltpu.VMEM)
SPAN = 4
LIMIT = 48 * 1024 * 1024


def up(value, multiple):
    return -(-value // multiple) * multiple


def pair_rows(rank):
    return rank * (rank // 2) + rank // 2


def halves(value):
    high = value.astype(jnp.bfloat16)
    return high, (value - high.astype(jnp.float32)).astype(jnp.bfloat16)


def write_pairs(twice, high, low, rank):
    first = twice[0:rank, :]
    for diag in range(rank // 2 + 1):
        count = rank if diag < rank // 2 else rank // 2
        rows = slice(diag * rank, diag * rank + count)
        high[rows, :], low[rows, :] = halves(first[0:count] * twice[diag : diag + count, :])


def unpack(packed, full, rank):
    for diag in range(rank // 2 + 1):
        base = diag * rank
        count = rank if diag < rank // 2 else rank // 2
        wrap = min(count, rank - diag)
        part = packed[base : base + wrap, :]
        full[pl.ds(diag, wrap, stride=rank + 1), :] = part
        if diag:
            full[pl.ds(diag * rank, wrap, stride=rank + 1), :] = part
        if wrap < count:
            part = packed[base + wrap : base + count, :]
            full[pl.ds(rank - diag, count - wrap, stride=rank + 1), :] = part
            full[pl.ds((rank - diag) * rank, count - wrap, stride=rank + 1), :] = part


def solve(fulls, targets, scaleds, rank):
    row = lax.broadcasted_iota(jnp.int32, (ROWS, LANES), 0)
    blocks = rank // ROWS
    targets = [[target[b * ROWS : (b + 1) * ROWS, :] for b in range(blocks)] for target in targets]
    pivots = [[jnp.zeros((ROWS, LANES), jnp.float32) for _ in range(blocks)] for _ in targets]
    tiles = range(len(targets))

    def part(k, b):
        return slice(k * rank + b * ROWS, k * rank + (b + 1) * ROWS)

    def reduced(t, k, b, stop):
        value = fulls[t][part(k, b), :]
        for j in range(stop):
            value = value - scaleds[t][part(j, b), :] * fulls[t][j * rank + k : j * rank + k + 1, :]
        return value

    for k in range(rank):
        first, place = k // ROWS, k % ROWS
        here = row == place
        for t in tiles:
            column = [reduced(t, k, b, k) for b in range(first, blocks)]
            inverse = 1.0 / column[0][place : place + 1, :]
            pivots[t][first] = jnp.where(here, column[0], pivots[t][first])
            known = targets[t][first][place : place + 1, :]
            for b in range(first, blocks):
                fulls[t][part(k, b), :] = column[b - first]
                factor = column[b - first] * inverse
                if b == first:
                    factor = jnp.where(here, 0.0, factor)
                scaleds[t][part(k, b), :] = factor
                targets[t][b] = targets[t][b] - factor * known
        if place == ROWS - 1:
            for t in tiles:
                for later in range(k + 1, rank):
                    fulls[t][part(later, first), :] = reduced(t, later, first, k + 1)
    for b in reversed(range(blocks)):
        for t in tiles:
            for k in reversed(range((b + 1) * ROWS, rank)):
                known = targets[t][k // ROWS][k % ROWS : k % ROWS + 1, :]
                targets[t][b] = targets[t][b] - fulls[t][part(k, b), :] * known
            targets[t][b] = targets[t][b] / pivots[t][b]
    return [jnp.concatenate(target, axis=0) for target in targets]


def dot(left, right, right_axis):
    return lax.dot_general(
        left, right, (((1,), (right_axis,)), ((), ())), preferred_element_type=jnp.float32
    )


def layout(rank, chunk, chunks):
    rows = up(chunk, ROWS)
    whole, rest = divmod(pair_rows(rank) + rank, LANES)
    beside = LANES // rest if rest else 1
    tail = -(-(chunks * rows // ROWS) // beside) if rest else 0
    return rows, whole, rest, beside, chunks * rows * whole + ROWS * tail


def spec_kernel(flux_hbm, weights_hbm, basis_hbm, own, other, *rest, chunk, span):
    sends, scratch = rest[:span], rest[span:]
    flux, weights, basis, twice, high, low, both, terms, last, tails, grams, sems = scratch
    rank, pixels = basis.shape
    spectra = weights.shape[0]
    half = own.shape[2]
    near = pl.multiple_of((lax.axis_index("spec") & 1) * half, LANES)
    far = pl.multiple_of(half - near, LANES)
    moves = [(basis_hbm, basis), (weights_hbm, weights), (flux_hbm, flux)]
    moves += [(flux_hbm.at[:, pl.ds(far, half)], other.at[1]), (weights_hbm.at[:, pl.ds(far, half)], other.at[0])]
    moves += [(flux_hbm.at[:, pl.ds(near, half)], own.at[1]), (weights_hbm.at[:, pl.ds(near, half)], own.at[0])]
    copies = [pltpu.make_async_copy(source, target, sems.at[k]) for k, (source, target) in enumerate(moves)]
    for copy in copies:
        copy.start()
    lead = pair_rows(rank)
    copies[0].wait()
    twice[0:rank, :] = basis[...]
    twice[rank:, :] = basis[...]
    terms[0:rank, :], terms[rank:, :] = halves(basis[...])
    write_pairs(twice, high, low, rank)
    copies[1].wait()
    both[0:spectra, :], both[spectra:, :] = halves(weights[...])
    part = dot(both[...], high[...], 1)
    packed = part[spectra:] + dot(both[0:spectra, :], low[...], 1) + part[0:spectra]
    copies[2].wait()
    flux[...] = weights[...] * flux[...]
    both[0:spectra, :], both[spectra:, :] = halves(flux[...])
    part = dot(both[...], terms[...], 1)
    target = part[spectra:, 0:rank] + part[0:spectra, rank:] + part[0:spectra, 0:rank]
    chunks = grams.shape[0] // span
    rows, whole, rest, beside, _ = layout(rank, chunk, chunks)
    last[:, 0 : rest - rank] = packed[:, lead + rank - rest :]
    last[:, rest - rank : rest] = target
    for k in range(grams.shape[0]):
        for t in range(whole):
            grams[k, t * rows : t * rows + chunk, :] = packed[k * chunk : (k + 1) * chunk, t * LANES : (t + 1) * LANES]
        tails[k, 0:chunk, 0:rest] = last[k * chunk : (k + 1) * chunk, 0:rest]
    for m, send in enumerate(sends):
        for h in range(chunks):
            source = h * span + (lax.axis_index("low") ^ m)
            send[h * whole * rows : (h + 1) * whole * rows, :] = grams[source, 0 : whole * rows, :]
            for g in range(rows // ROWS):
                slot = h * (rows // ROWS) + g
                base = chunks * whole * rows + slot // beside * ROWS
                lanes = slice(slot % beside * rest, (slot % beside + 1) * rest)
                send[base : base + ROWS, lanes] = tails[source, g * ROWS : (g + 1) * ROWS, 0:rest]
    for copy in copies[3:]:
        copy.wait()


def add_kernel(*refs):
    total = refs[0][...]
    for term in refs[1:-1]:
        total = total + term[...]
    refs[-1][...] = total


def coeff_kernel(sums, arrived, out, packed, full, scaled, *, rank, chunk, chunks):
    total = sums[...] + arrived[...]
    rows, whole, rest, beside, _ = layout(rank, chunk, chunks)
    filler = jnp.ones((LANES - chunks * rows, LANES), jnp.float32)
    for t in range(whole):
        block = [total[(h * whole + t) * rows : (h * whole + t + 1) * rows] for h in range(chunks)]
        packed[t * LANES : (t + 1) * LANES, :] = jnp.concatenate(block + [filler], axis=0).T
    groups = []
    for slot in range(chunks * rows // ROWS):
        base = chunks * rows * whole + slot // beside * ROWS
        group = total[base : base + ROWS]
        groups.append(pltpu.roll(group, LANES - slot % beside * rest, 1) if slot % beside else group)
    packed[whole * LANES :, :] = jnp.concatenate(groups + [filler], axis=0).T
    lead = pair_rows(rank)
    unpack(packed, full, rank)
    (solved,) = solve([full], [packed[lead : lead + rank, :]], [scaled], rank)
    lane = lax.broadcasted_iota(jnp.int32, (ROWS, LANES), 1)
    for h in range(chunks):
        tile = jnp.zeros((ROWS, LANES), jnp.float32)
        for a in range(rank // ROWS):
            part = solved[a * ROWS : (a + 1) * ROWS, :]
            shift = (a * chunk - h * rows) % LANES
            if shift:
                part = pltpu.roll(part, shift, 1)
            tile = jnp.where((lane >= a * chunk) & (lane < (a + 1) * chunk), part, tile)
        for k in range(out.shape[0]):
            out[k, h] = tile


def terms_kernel(*refs, peers):
    picks, (high, low) = refs[:peers], refs[peers:]
    spectra = picks[0].shape[1]
    for q, pick in enumerate(picks):
        rows = pl.ds(pl.multiple_of((lax.axis_index("spec") ^ q) * spectra, 16), spectra)
        high[0, rows, :], low[0, rows, :] = halves(pick[0])
        high[1, rows, :], low[1, rows, :] = halves(pick[0] * pick[1])


def pixel_kernel(tiles, high, low, out, twice, pairs, full, scaled, *, peers, rank, chunk):
    spectra = high.shape[1] // peers
    half = high.shape[2]
    group = spectra // chunk
    lane = lax.broadcasted_iota(jnp.int32, (ROWS, LANES), 1)
    width = twice.shape[1]
    for a in range(rank // ROWS):
        columns = [jnp.zeros((ROWS, LANES), jnp.float32) for _ in range(width // LANES)]
        for q in range(peers):
            for k in range(group):
                part = tiles[q * SPAN + k % SPAN, k // SPAN]
                start = q * spectra + k * chunk
                shift = (start - a * chunk) % LANES
                if shift:
                    part = pltpu.roll(part, shift, 1)
                for t in range(start // LANES, (start + chunk - 1) // LANES + 1):
                    begin, end = max(start - t * LANES, 0), min(start + chunk - t * LANES, LANES)
                    columns[t] = jnp.where((lane >= begin) & (lane < end), part, columns[t])
        for t, column in enumerate(columns):
            twice[a * ROWS : (a + 1) * ROWS, t * LANES : (t + 1) * LANES] = column
            twice[rank + a * ROWS : rank + (a + 1) * ROWS, t * LANES : (t + 1) * LANES] = column
    depth = high.shape[1]
    lead = pair_rows(rank)
    write_pairs(twice, pairs.at[0:lead], pairs.at[lead : 2 * lead], rank)
    part = dot(pairs[:, 0:depth], high[0], 0)
    packed = part[lead:] + dot(pairs[0:lead, 0:depth], low[0], 0) + part[0:lead]
    terms = jnp.concatenate(halves(twice[0:rank, 0:depth]), axis=0)
    part = dot(terms, high[1], 0)
    target = part[rank:] + dot(terms[0:rank], low[1], 0) + part[0:rank]
    tiles = range(half // LANES)
    for t in tiles:
        unpack(packed[:, t * LANES : (t + 1) * LANES], full.at[t], rank)
    solved = solve(
        [full.at[t] for t in tiles],
        [target[:, t * LANES : (t + 1) * LANES] for t in tiles],
        [scaled.at[t] for t in tiles],
        rank,
    )
    for t in tiles:
        out[:, t * LANES : (t + 1) * LANES] = solved[t]


def place_kernel(own, other, out):
    half = own.shape[1]
    low = pl.multiple_of((lax.axis_index("spec") & 1) * half, LANES)
    out[:, pl.ds(low, half)] = own[...]
    out[:, pl.ds(pl.multiple_of(half - low, LANES), half)] = other[...]


def scratch_shape(sizes):
    if not isinstance(sizes, tuple):
        return sizes
    if sizes[0] is jnp.bfloat16:
        return pltpu.VMEM(sizes[1:], jnp.bfloat16)
    return pltpu.VMEM(sizes, jnp.float32)


def call(kernel, outs, scratch, *args, space=pltpu.VMEM):
    return pl.pallas_call(
        kernel,
        out_shape=outs,
        in_specs=[pl.BlockSpec(memory_space=space)] * len(args),
        out_specs=jax.tree.map(lambda _: VMEM, outs),
        scratch_shapes=[scratch_shape(s) for s in scratch],
        compiler_params=pltpu.CompilerParams(vmem_limit_bytes=LIMIT),
    )(*args)


def shape(*sizes):
    return jax.ShapeDtypeStruct(sizes, jnp.float32)


def local(peers, groups, spectra_flux, pixel_weights, old_basis):
    spectra, pixels = pixel_weights.shape
    rank = old_basis.shape[0]
    half, chunk = pixels // 2, spectra // groups
    lead = pair_rows(rank)
    wide = up(lead + rank, LANES)
    chunks = groups // SPAN
    kept = shape(layout(rank, chunk, chunks)[-1], LANES)
    half_type = jnp.bfloat16
    inputs = [pltpu.with_memory_space_constraint(a, pltpu.HBM) for a in (spectra_flux, pixel_weights, old_basis)]

    def swap(value, axis, mask):
        axis, size = ("spec", peers) if axis == "spec" else (("high", "low"), groups)
        return lax.ppermute(value, axis, [(s, s ^ mask) for s in range(size)])

    own, other, *sends = call(
        functools.partial(spec_kernel, chunk=chunk, span=SPAN),
        [shape(2, spectra, half)] * 2 + [kept] * SPAN,
        [
            (spectra, pixels),
            (spectra, pixels),
            (rank, pixels),
            (2 * rank, pixels),
            (half_type, lead, pixels),
            (half_type, lead, pixels),
            (half_type, 2 * spectra, pixels),
            (half_type, 2 * rank, pixels),
            (spectra, LANES),
            (groups, up(chunk, ROWS), LANES),
            (groups, up(chunk, ROWS) * (wide // LANES), LANES),
            pltpu.SemaphoreType.DMA((7,)),
        ],
        *inputs,
        space=pl.ANY,
    )
    arrived = [swap(sends[m], "pix", m) for m in range(SPAN - 1, 0, -1)]
    picks = [own] + [swap(other if q & 1 else own, "spec", q) for q in range(1, peers)]
    sums = call(add_kernel, kept, [], sends[0], *arrived)
    reach = SPAN
    while 2 * reach < groups:
        sums = call(add_kernel, kept, [], sums, swap(sums, "pix", reach))
        reach *= 2
    tiles = call(
        functools.partial(coeff_kernel, rank=rank, chunk=chunk, chunks=chunks),
        shape(peers * SPAN, groups // SPAN, ROWS, LANES),
        [(wide, LANES), (rank * rank, LANES), (rank * rank, LANES)],
        sums,
        swap(sums, "pix", reach),
    )
    tiles = lax.all_to_all(tiles, ("spec", "low"), 0, 0)
    depth = peers * spectra
    terms = [jax.ShapeDtypeStruct((2, depth, half), jnp.bfloat16)] * 2
    high, low = call(functools.partial(terms_kernel, peers=peers), terms, [], *picks)
    mine = call(
        functools.partial(pixel_kernel, peers=peers, rank=rank, chunk=chunk),
        shape(rank, half),
        [
            (2 * rank, up(depth, LANES)),
            (half_type, 2 * lead, up(depth, LANES)),
            (half // LANES, rank * rank, LANES),
            (half // LANES, rank * rank, LANES),
        ],
        tiles,
        high,
        low,
    )
    return call(place_kernel, shape(rank, pixels), [], mine, swap(mine, "spec", 1))


def solution(mesh):
    peers, groups = mesh.shape["spec"], mesh.shape["pix"]
    split = jax.sharding.Mesh(mesh.devices.reshape(peers, groups // SPAN, SPAN), ("spec", "high", "low"))
    pix = ("high", "low")
    body = functools.partial(local, peers, groups)
    placed = (P("spec", pix), P("spec", pix), P(None, pix))
    return jax.shard_map(body, mesh=split, in_specs=placed, out_specs=P(None, pix), check_vma=False)
```

```python
import functools

import jax
import jax.numpy as jnp
from jax import lax
from jax.experimental import pallas as pl
from jax.experimental.pallas import tpu as pltpu
from jax.sharding import PartitionSpec as P

LANES = 128
ROWS = 8
VMEM = pl.BlockSpec(memory_space=pltpu.VMEM)
SPAN = 4
LIMIT = 48 * 1024 * 1024


def up(value, multiple):
    return -(-value // multiple) * multiple


def pair_rows(rank):
    return rank * (rank // 2) + rank // 2


def halves(value):
    high = value.astype(jnp.bfloat16)
    return high, (value - high.astype(jnp.float32)).astype(jnp.bfloat16)


def write_pairs(twice, high, low, rank):
    first = twice[0:rank, :]
    for diag in range(rank // 2 + 1):
        count = rank if diag < rank // 2 else rank // 2
        rows = slice(diag * rank, diag * rank + count)
        high[rows, :], low[rows, :] = halves(first[0:count] * twice[diag : diag + count, :])


def unpack(packed, full, rank):
    for diag in range(rank // 2 + 1):
        base = diag * rank
        count = rank if diag < rank // 2 else rank // 2
        wrap = min(count, rank - diag)
        part = packed[base : base + wrap, :]
        full[pl.ds(diag, wrap, stride=rank + 1), :] = part
        if diag:
            full[pl.ds(diag * rank, wrap, stride=rank + 1), :] = part
        if wrap < count:
            part = packed[base + wrap : base + count, :]
            full[pl.ds(rank - diag, count - wrap, stride=rank + 1), :] = part
            full[pl.ds((rank - diag) * rank, count - wrap, stride=rank + 1), :] = part


def solve(fulls, targets, scaleds, rank):
    row = lax.broadcasted_iota(jnp.int32, (ROWS, LANES), 0)
    blocks = rank // ROWS
    targets = [[target[b * ROWS : (b + 1) * ROWS, :] for b in range(blocks)] for target in targets]
    pivots = [[jnp.zeros((ROWS, LANES), jnp.float32) for _ in range(blocks)] for _ in targets]
    tiles = range(len(targets))

    def part(k, b):
        return slice(k * rank + b * ROWS, k * rank + (b + 1) * ROWS)

    def reduced(t, k, b, stop):
        value = fulls[t][part(k, b), :]
        for j in range(stop):
            value = value - scaleds[t][part(j, b), :] * fulls[t][j * rank + k : j * rank + k + 1, :]
        return value

    for k in range(rank):
        first, place = k // ROWS, k % ROWS
        here = row == place
        for t in tiles:
            column = [reduced(t, k, b, k) for b in range(first, blocks)]
            inverse = 1.0 / column[0][place : place + 1, :]
            pivots[t][first] = jnp.where(here, column[0], pivots[t][first])
            known = targets[t][first][place : place + 1, :]
            for b in range(first, blocks):
                fulls[t][part(k, b), :] = column[b - first]
                factor = column[b - first] * inverse
                if b == first:
                    factor = jnp.where(here, 0.0, factor)
                scaleds[t][part(k, b), :] = factor
                targets[t][b] = targets[t][b] - factor * known
        if place == ROWS - 1:
            for t in tiles:
                for later in range(k + 1, rank):
                    fulls[t][part(later, first), :] = reduced(t, later, first, k + 1)
    for b in reversed(range(blocks)):
        for t in tiles:
            for k in reversed(range((b + 1) * ROWS, rank)):
                known = targets[t][k // ROWS][k % ROWS : k % ROWS + 1, :]
                targets[t][b] = targets[t][b] - fulls[t][part(k, b), :] * known
            targets[t][b] = targets[t][b] / pivots[t][b]
    return [jnp.concatenate(target, axis=0) for target in targets]


def dot(left, right, right_axis):
    return lax.dot_general(
        left, right, (((1,), (right_axis,)), ((), ())), preferred_element_type=jnp.float32
    )


def layout(rank, chunk, chunks):
    rows = up(chunk, ROWS)
    whole, rest = divmod(pair_rows(rank) + rank, LANES)
    beside = LANES // rest if rest else 1
    tail = -(-(chunks * rows // ROWS) // beside) if rest else 0
    return rows, whole, rest, beside, chunks * rows * whole + ROWS * tail


def spec_kernel(flux_hbm, weights_hbm, basis_hbm, own, other, *rest, chunk, span):
    sends, scratch = rest[:span], rest[span:]
    flux, weights, basis, twice, high, low, both, terms, last, tails, grams, sems = scratch
    rank, pixels = basis.shape
    spectra = weights.shape[0]
    half = own.shape[2]
    near = pl.multiple_of((lax.axis_index("spec") & 1) * half, LANES)
    far = pl.multiple_of(half - near, LANES)
    moves = [(basis_hbm, basis), (weights_hbm, weights), (flux_hbm, flux)]
    moves += [(flux_hbm.at[:, pl.ds(far, half)], other.at[1]), (weights_hbm.at[:, pl.ds(far, half)], other.at[0])]
    moves += [(flux_hbm.at[:, pl.ds(near, half)], own.at[1]), (weights_hbm.at[:, pl.ds(near, half)], own.at[0])]
    copies = [pltpu.make_async_copy(source, target, sems.at[k]) for k, (source, target) in enumerate(moves)]
    for copy in copies:
        copy.start()
    lead = pair_rows(rank)
    copies[0].wait()
    twice[0:rank, :] = basis[...]
    twice[rank:, :] = basis[...]
    terms[0:rank, :], terms[rank:, :] = halves(basis[...])
    write_pairs(twice, high, low, rank)
    copies[1].wait()
    both[0:spectra, :], both[spectra:, :] = halves(weights[...])
    part = dot(both[...], high[...], 1)
    packed = part[spectra:] + dot(both[0:spectra, :], low[...], 1) + part[0:spectra]
    copies[2].wait()
    flux[...] = weights[...] * flux[...]
    both[0:spectra, :], both[spectra:, :] = halves(flux[...])
    part = dot(both[...], terms[...], 1)
    target = part[spectra:, 0:rank] + part[0:spectra, rank:] + part[0:spectra, 0:rank]
    chunks = grams.shape[0] // span
    rows, whole, rest, beside, _ = layout(rank, chunk, chunks)
    last[:, 0 : rest - rank] = packed[:, lead + rank - rest :]
    last[:, rest - rank : rest] = target
    for k in range(grams.shape[0]):
        for t in range(whole):
            grams[k, t * rows : t * rows + chunk, :] = packed[k * chunk : (k + 1) * chunk, t * LANES : (t + 1) * LANES]
        tails[k, 0:chunk, 0:rest] = last[k * chunk : (k + 1) * chunk, 0:rest]
    for m, send in enumerate(sends):
        for h in range(chunks):
            source = h * span + (lax.axis_index("low") ^ m)
            send[h * whole * rows : (h + 1) * whole * rows, :] = grams[source, 0 : whole * rows, :]
            for g in range(rows // ROWS):
                slot = h * (rows // ROWS) + g
                base = chunks * whole * rows + slot // beside * ROWS
                lanes = slice(slot % beside * rest, (slot % beside + 1) * rest)
                send[base : base + ROWS, lanes] = tails[source, g * ROWS : (g + 1) * ROWS, 0:rest]
    for copy in copies[3:]:
        copy.wait()


def add_kernel(*refs):
    total = refs[0][...]
    for term in refs[1:-1]:
        total = total + term[...]
    refs[-1][...] = total


def coeff_kernel(sums, arrived, out, packed, full, scaled, *, rank, chunk, chunks):
    total = sums[...] + arrived[...]
    rows, whole, rest, beside, _ = layout(rank, chunk, chunks)
    filler = jnp.ones((LANES - chunks * rows, LANES), jnp.float32)
    for t in range(whole):
        block = [total[(h * whole + t) * rows : (h * whole + t + 1) * rows] for h in range(chunks)]
        packed[t * LANES : (t + 1) * LANES, :] = jnp.concatenate(block + [filler], axis=0).T
    groups = []
    for slot in range(chunks * rows // ROWS):
        base = chunks * rows * whole + slot // beside * ROWS
        group = total[base : base + ROWS]
        groups.append(pltpu.roll(group, LANES - slot % beside * rest, 1) if slot % beside else group)
    packed[whole * LANES :, :] = jnp.concatenate(groups + [filler], axis=0).T
    lead = pair_rows(rank)
    unpack(packed, full, rank)
    (solved,) = solve([full], [packed[lead : lead + rank, :]], [scaled], rank)
    lane = lax.broadcasted_iota(jnp.int32, (ROWS, LANES), 1)
    for h in range(chunks):
        tile = jnp.zeros((ROWS, LANES), jnp.float32)
        for a in range(rank // ROWS):
            part = solved[a * ROWS : (a + 1) * ROWS, :]
            shift = (a * chunk - h * rows) % LANES
            if shift:
                part = pltpu.roll(part, shift, 1)
            tile = jnp.where((lane >= a * chunk) & (lane < (a + 1) * chunk), part, tile)
        for k in range(out.shape[0]):
            out[k, h] = tile


def terms_kernel(*refs, peers):
    picks, (high, low) = refs[:peers], refs[peers:]
    spectra = picks[0].shape[1]
    for q, pick in enumerate(picks):
        rows = pl.ds(pl.multiple_of((lax.axis_index("spec") ^ q) * spectra, 16), spectra)
        high[0, rows, :], low[0, rows, :] = halves(pick[0])
        high[1, rows, :], low[1, rows, :] = halves(pick[0] * pick[1])


def pixel_kernel(tiles, high, low, out, twice, pairs, full, scaled, *, peers, rank, chunk):
    spectra = high.shape[1] // peers
    half = high.shape[2]
    group = spectra // chunk
    lane = lax.broadcasted_iota(jnp.int32, (ROWS, LANES), 1)
    width = twice.shape[1]
    for a in range(rank // ROWS):
        columns = [jnp.zeros((ROWS, LANES), jnp.float32) for _ in range(width // LANES)]
        for q in range(peers):
            for k in range(group):
                part = tiles[q * SPAN + k % SPAN, k // SPAN]
                start = q * spectra + k * chunk
                shift = (start - a * chunk) % LANES
                if shift:
                    part = pltpu.roll(part, shift, 1)
                for t in range(start // LANES, (start + chunk - 1) // LANES + 1):
                    begin, end = max(start - t * LANES, 0), min(start + chunk - t * LANES, LANES)
                    columns[t] = jnp.where((lane >= begin) & (lane < end), part, columns[t])
        for t, column in enumerate(columns):
            twice[a * ROWS : (a + 1) * ROWS, t * LANES : (t + 1) * LANES] = column
            twice[rank + a * ROWS : rank + (a + 1) * ROWS, t * LANES : (t + 1) * LANES] = column
    depth = high.shape[1]
    lead = pair_rows(rank)
    write_pairs(twice, pairs.at[0:lead], pairs.at[lead : 2 * lead], rank)
    part = dot(pairs[:, 0:depth], high[0], 0)
    packed = part[lead:] + dot(pairs[0:lead, 0:depth], low[0], 0) + part[0:lead]
    terms = jnp.concatenate(halves(twice[0:rank, 0:depth]), axis=0)
    part = dot(terms, high[1], 0)
    target = part[rank:] + dot(terms[0:rank], low[1], 0) + part[0:rank]
    tiles = range(half // LANES)
    for t in tiles:
        unpack(packed[:, t * LANES : (t + 1) * LANES], full.at[t], rank)
    solved = solve(
        [full.at[t] for t in tiles],
        [target[:, t * LANES : (t + 1) * LANES] for t in tiles],
        [scaled.at[t] for t in tiles],
        rank,
    )
    for t in tiles:
        out[:, t * LANES : (t + 1) * LANES] = solved[t]


def place_kernel(own, other, out):
    half = own.shape[1]
    low = pl.multiple_of((lax.axis_index("spec") & 1) * half, LANES)
    out[:, pl.ds(low, half)] = own[...]
    out[:, pl.ds(pl.multiple_of(half - low, LANES), half)] = other[...]


def scratch_shape(sizes):
    if not isinstance(sizes, tuple):
        return sizes
    if sizes[0] is jnp.bfloat16:
        return pltpu.VMEM(sizes[1:], jnp.bfloat16)
    return pltpu.VMEM(sizes, jnp.float32)


def call(kernel, outs, scratch, *args, space=pltpu.VMEM):
    return pl.pallas_call(
        kernel,
        out_shape=outs,
        in_specs=[pl.BlockSpec(memory_space=space)] * len(args),
        out_specs=jax.tree.map(lambda _: VMEM, outs),
        scratch_shapes=[scratch_shape(s) for s in scratch],
        compiler_params=pltpu.CompilerParams(vmem_limit_bytes=LIMIT),
    )(*args)


def shape(*sizes):
    return jax.ShapeDtypeStruct(sizes, jnp.float32)


def local(peers, groups, spectra_flux, pixel_weights, old_basis):
    spectra, pixels = pixel_weights.shape
    rank = old_basis.shape[0]
    half, chunk = pixels // 2, spectra // groups
    lead = pair_rows(rank)
    wide = up(lead + rank, LANES)
    chunks = groups // SPAN
    kept = shape(layout(rank, chunk, chunks)[-1], LANES)
    half_type = jnp.bfloat16
    inputs = [pltpu.with_memory_space_constraint(a, pltpu.HBM) for a in (spectra_flux, pixel_weights, old_basis)]

    def swap(value, axis, mask):
        axis, size = ("spec", peers) if axis == "spec" else (("high", "low"), groups)
        return lax.ppermute(value, axis, [(s, s ^ mask) for s in range(size)])

    own, other, *sends = call(
        functools.partial(spec_kernel, chunk=chunk, span=SPAN),
        [shape(2, spectra, half)] * 2 + [kept] * SPAN,
        [
            (spectra, pixels),
            (spectra, pixels),
            (rank, pixels),
            (2 * rank, pixels),
            (half_type, lead, pixels),
            (half_type, lead, pixels),
            (half_type, 2 * spectra, pixels),
            (half_type, 2 * rank, pixels),
            (spectra, LANES),
            (groups, up(chunk, ROWS), LANES),
            (groups, up(chunk, ROWS) * (wide // LANES), LANES),
            pltpu.SemaphoreType.DMA((7,)),
        ],
        *inputs,
        space=pl.ANY,
    )
    arrived = [swap(sends[m], "pix", m) for m in sorted(range(1, SPAN), key=lambda m: (1 - m % 2, m))]
    picks = [own] + [swap(other if q & 1 else own, "spec", q) for q in range(1, peers)]
    sums = call(add_kernel, kept, [], sends[0], *arrived)
    reach = SPAN
    while 2 * reach < groups:
        sums = call(add_kernel, kept, [], sums, swap(sums, "pix", reach))
        reach *= 2
    tiles = call(
        functools.partial(coeff_kernel, rank=rank, chunk=chunk, chunks=chunks),
        shape(peers * SPAN, groups // SPAN, ROWS, LANES),
        [(wide, LANES), (rank * rank, LANES), (rank * rank, LANES)],
        sums,
        swap(sums, "pix", reach),
    )
    tiles = lax.all_to_all(tiles, ("spec", "low"), 0, 0)
    depth = peers * spectra
    terms = [jax.ShapeDtypeStruct((2, depth, half), jnp.bfloat16)] * 2
    high, low = call(functools.partial(terms_kernel, peers=peers), terms, [], *picks)
    mine = call(
        functools.partial(pixel_kernel, peers=peers, rank=rank, chunk=chunk),
        shape(rank, half),
        [
            (2 * rank, up(depth, LANES)),
            (half_type, 2 * lead, up(depth, LANES)),
            (half // LANES, rank * rank, LANES),
            (half // LANES, rank * rank, LANES),
        ],
        tiles,
        high,
        low,
    )
    return call(place_kernel, shape(rank, pixels), [], mine, swap(mine, "spec", 1))


def solution(mesh):
    peers, groups = mesh.shape["spec"], mesh.shape["pix"]
    split = jax.sharding.Mesh(mesh.devices.reshape(peers, groups // SPAN, SPAN), ("spec", "high", "low"))
    pix = ("high", "low")
    body = functools.partial(local, peers, groups)
    placed = (P("spec", pix), P("spec", pix), P(None, pix))
    return jax.shard_map(body, mesh=split, in_specs=placed, out_specs=P(None, pix), check_vma=False)
```
